256 devices in a mesh: seq: 32 (over y, z), head: 8 (over x, core).
Axes of the slice: x: 4, y: 4, z: 8, core: 2. Of those that a mesh axis runs over, the one named last changes fastest.
Arguments:
- teacher_query: bfloat16 [4096, 4096], P('seq', 'head')
- teacher_key: bfloat16 [4096, 4096], P('seq', 'head')
- teacher_value: bfloat16 [4096, 4096], P('seq', 'head')
- student_hidden: bfloat16 [4096, 2048], P('seq')
- weight_query: bfloat16 [2048, 1024], P(None, 'head'), may hold values from -0.125 to 0.125
- weight_key: bfloat16 [2048, 1024], P(None, 'head'), may hold values from -0.125 to 0.125
- weight_value: bfloat16 [2048, 1024], P(None, 'head'), may hold values from -0.125 to 0.125
- teacher_shift: int32 [1], replicated, may hold values from 128 to 383
- student_shift: int32 [1], replicated, may hold values from 32 to 95
- segment_lengths: int32 [4], replicated, may hold values from 1 to 3072, 4096 in all
Outputs:
- mean_divergence: float32 [], replicated
- gradient_query: bfloat16 [2048, 1024], P('seq', 'head')
- gradient_key: bfloat16 [2048, 1024], P('seq', 'head')
- gradient_value: bfloat16 [2048, 1024], P('seq', 'head')
The draws below stay inside these ranges and needn't reach their ends.
Inputs may be any that keep to these rules, and one draw needn't show every extreme that they name: teacher_shift lies in 0 .. 511. student_shift lies in 0 .. 127. `segment_lengths`: the lengths sum to 4096; the largest is exactly 3072.
All inputs are finite; a program needn't handle non-finite values.
Results may differ from the reference program's by a relative error of at most 0.0054.
Values may be sent and summed in bfloat16 or wider, within the bound.
A program may use at most 128 MiB of HBM per device.

```python
import math
import jax
import jax.numpy as jnp
import numpy as np
from jax import lax

SEQ = 4096
DS = 2048
RT = 256
RS = 64
RH_DEV = 2
RHEADS = 16
TW = 4096
SW = 1024
DOCS = 4


def token_factors(key):
    return jnp.clip(jax.random.normal(key, (SEQ, 8), jnp.float32), -4.0, 4.0)


def shaped_rows(token_mix, key, width, common, spread):
    key_dirs, key_noise = jax.random.split(key, 2)
    directions = jnp.clip(jax.random.normal(key_dirs, (8, width), jnp.float32), -4.0, 4.0)
    noise_vals = jnp.clip(jax.random.normal(key_noise, (SEQ, width), jnp.float32), -4.0, 4.0)
    factor = math.sqrt(common / 8.0)
    values = math.sqrt(spread) * noise_vals
    for member in range(8):
        values = values + factor * token_mix[:, member:member + 1] * directions[member][None, :]
    return values


def draw_teacher_query(key, part):
    token_mix = token_factors(key)
    key = jax.random.fold_in(key, 11)
    return shaped_rows(token_mix, key, TW, 0.44, 0.15).astype(jnp.bfloat16)


def draw_teacher_key(key, part):
    token_mix = token_factors(key)
    key = jax.random.fold_in(key, 12)
    return shaped_rows(token_mix, key, TW, 0.44, 0.15).astype(jnp.bfloat16)


def draw_teacher_value(key, part):
    token_mix = token_factors(key)
    key = jax.random.fold_in(key, 13)
    return shaped_rows(token_mix, key, TW, 0.44, 0.15).astype(jnp.bfloat16)


def draw_student_hidden(key, part):
    token_mix = token_factors(key)
    key = jax.random.fold_in(key, 14)
    return shaped_rows(token_mix, key, DS, 0.7, 0.3).astype(jnp.bfloat16)


def shard_levels(stream_key, shape, cuts, low, largest):
    gain = 1.0
    for position, parts in cuts:
        heights = jax.random.uniform(jax.random.fold_in(jax.random.fold_in(stream_key, 6), position), (parts,), jnp.float32, low / len(cuts), largest / len(cuts))
        gain = gain * jnp.repeat(jnp.exp(heights), shape[position] // parts).reshape((-1,) + (1,) * (len(shape) - 1 - position))
    return gain


def length_profile(count, total, limit, slope):
    portions = [(1 << 20) // math.isqrt(grade ** slope) + 1 for grade in range(2, count + 1)]
    surplus, holding = total - limit - (count - 1), [1] * (count - 1)
    while surplus > 0:
        free = [i for i in range(count - 1) if holding[i] < limit]
        mass, budget = sum([portions[i] for i in free]), surplus
        for i in free:
            more = min(limit - holding[i], max(1, budget * portions[i] // mass), surplus)
            holding[i] = holding[i] + more
            surplus = surplus - more
    return np.array([limit] + holding)


def uneven_parts(own_key, number_of, total, bound, skew):
    if number_of == 2:
        one = jax.random.randint(own_key, (), max(1, total - bound), min(bound, total - 1) + 1)
        return jnp.stack([one, total - one])
    lengths = jnp.asarray(length_profile(number_of, total, bound, skew), jnp.int32)
    pairs = (number_of - 1) // 2
    giver, receiver = lengths[1:1 + 2 * pairs:2], lengths[2:2 + 2 * pairs:2]
    room = jnp.minimum(giver - 1, bound - receiver)
    passed = jax.random.randint(jax.random.fold_in(own_key, 1), (pairs,), 0, 1 << 20) % (room + 1)
    lengths = lengths.at[1:1 + 2 * pairs:2].set(giver - passed).at[2:2 + 2 * pairs:2].set(receiver + passed)
    return lengths[jax.random.permutation(jax.random.fold_in(own_key, 2), number_of)]


def scatter_about(rng, dims, deviation, most, cuts=(), kind=jnp.bfloat16):
    values = jax.random.normal(rng, dims, jnp.float32) * deviation
    if len(cuts) > 0:
        values = shard_levels(rng, dims, cuts, -0.22, 0.18) * values
    return jnp.clip(values, min=-most, max=most).astype(kind)


def setup_inputs(seed: int = 0) -> dict:
    keys = jax.random.split(jax.random.key(seed), 11)
    teacher_query = draw_teacher_query(jax.random.fold_in(keys[10], 71), 0)
    teacher_key = draw_teacher_key(jax.random.fold_in(keys[10], 71), 0)
    teacher_value = draw_teacher_value(jax.random.fold_in(keys[10], 71), 0)
    student_hidden = draw_student_hidden(jax.random.fold_in(keys[10], 71), 0)
    weight_query = scatter_about(keys[4], (DS, SW), DS ** -0.5, 0.125, ((1, 8),))
    weight_key = scatter_about(keys[5], (DS, SW), DS ** -0.5, 0.125, ((1, 8),))
    weight_value = scatter_about(keys[6], (DS, SW), DS ** -0.5, 0.125, ((1, 8),))
    teacher_shift = jax.random.randint(keys[7], (1,), RH_DEV * RT // 4, 3 * RH_DEV * RT // 4).astype(jnp.int32)
    student_shift = jax.random.randint(keys[8], (1,), RH_DEV * RS // 4, 3 * RH_DEV * RS // 4).astype(jnp.int32)
    segment_lengths = uneven_parts(keys[9], DOCS, SEQ, 3 * SEQ // 4, 1).astype(jnp.int32)
    return dict(teacher_query=teacher_query, teacher_key=teacher_key, teacher_value=teacher_value, student_hidden=student_hidden, weight_query=weight_query, weight_key=weight_key, weight_value=weight_value, teacher_shift=teacher_shift, student_shift=student_shift, segment_lengths=segment_lengths)


NEG = -1e+30

def document_index(positions, segment_lengths):
    ends = jnp.cumsum(segment_lengths)
    return lax.optimization_barrier(jnp.sum((positions[:, None] >= ends[None, :]).astype(jnp.int32), axis=1))

def allowed_pairs(rows, cols, segment_lengths):
    same = document_index(rows, segment_lengths)[:, None] == document_index(cols, segment_lengths)[None, :]
    return jnp.logical_and(same, cols[None, :] <= rows[:, None])

def row_stats(scores, allowed):
    masked = jnp.where(allowed, scores, NEG)
    peak = lax.optimization_barrier(jnp.max(masked, axis=-1, keepdims=True))
    total = lax.optimization_barrier(jnp.sum(jnp.exp(masked - peak), axis=-1, keepdims=True))
    return (peak, total)

def normalize(scores, allowed, peak, total):
    masked = jnp.where(allowed, scores, NEG)
    prob = jnp.exp(masked - peak) / total
    logp = masked - peak - jnp.log(total)
    return (prob, logp)

def split_heads(matrix, shift, width):
    rolled = jnp.roll(matrix, -shift, axis=1)
    return jnp.transpose(rolled.reshape(matrix.shape[0], -1, width), (1, 0, 2))

def merge_heads(pieces, shift):
    flat = jnp.transpose(pieces, (1, 0, 2)).reshape(pieces.shape[1], -1)
    return jnp.roll(flat, shift, axis=1)

def reference(teacher_query, teacher_key, teacher_value, student_hidden, weight_query, weight_key, weight_value, teacher_shift, student_shift, segment_lengths):
    positions = jnp.arange(SEQ, dtype=jnp.int32)
    allowed = allowed_pairs(positions, positions, segment_lengths)
    coef = 1.0 / (3 * RHEADS)
    scale_t = 1.0 / math.sqrt(RT)
    scale_s = 1.0 / math.sqrt(RS)

    def one_head(pair):
        a_t, a_s = pair
        st = jnp.dot(a_t, a_t.T, preferred_element_type=jnp.float32) * scale_t
        ss = jnp.dot(a_s, a_s.T, preferred_element_type=jnp.float32) * scale_s
        peak_t, total_t = row_stats(st, allowed)
        peak_s, total_s = row_stats(ss, allowed)
        prob_t, logp_t = normalize(st, allowed, peak_t, total_t)
        prob_s, logp_s = normalize(ss, allowed, peak_s, total_s)
        kl_sum = jnp.sum(jnp.where(allowed, prob_t * (logp_t - logp_s), jnp.float32(0.0)))
        gmat = (jnp.where(allowed, prob_s - prob_t, jnp.float32(0.0)) * coef).astype(jnp.bfloat16)
        near = jnp.dot(gmat, a_s, preferred_element_type=jnp.float32)
        far = jnp.dot(gmat.T, a_s, preferred_element_type=jnp.float32)
        return (kl_sum, (near + far) * scale_s)
    divergence = jnp.float32(0.0)
    grads = []
    for teacher, weight in ((teacher_query, weight_query), (teacher_key, weight_key), (teacher_value, weight_value)):
        student = jnp.dot(student_hidden, weight, preferred_element_type=jnp.float32).astype(jnp.bfloat16)
        heads_t = split_heads(teacher, teacher_shift[0], RT)
        heads_s = split_heads(student, student_shift[0], RS)
        kls, pieces = lax.map(one_head, (heads_t, heads_s))
        divergence = divergence + jnp.sum(kls)
        dstudent = merge_heads(pieces, student_shift[0]).astype(jnp.bfloat16)
        grads.append(jnp.dot(student_hidden.T, dstudent, preferred_element_type=jnp.float32).astype(jnp.bfloat16))
    mean_divergence = divergence / (3 * RHEADS * SEQ)
    return (mean_divergence, grads[0], grads[1], grads[2])
```

```python
import functools
import math

import jax
import jax.numpy as jnp
from jax import lax
from jax.experimental import pallas as pl
from jax.experimental.pallas import tpu as pltpu
from jax.sharding import PartitionSpec as P

MESH = pl.DeviceIdType.MESH
NEG = -1e30
TOK = 128
NZ = 8
NY = 4
PAIRS = 6
SLOTS = NY * NZ
PIECE = 320
ROWS = 256
CHUNK = 512
KEYS = SLOTS * TOK
F32 = jnp.float32
BF16 = jnp.bfloat16


def place():
    seq = lax.axis_index("seq")
    head = lax.axis_index("head")
    return seq, head, seq // NZ, seq % NZ, head // 2, head % 2


def greet(peers):
    barrier = pltpu.get_barrier_semaphore()
    for peer in peers:
        pl.semaphore_signal(barrier, inc=1, device_id=peer, device_id_type=MESH)
    return lambda: pl.semaphore_wait(barrier, len(peers))


def remote(src, dst, send, recv, device):
    return pltpu.make_async_remote_copy(
        src_ref=src, dst_ref=dst, send_sem=send, recv_sem=recv, device_id=device, device_id_type=MESH
    )


def swap_halves(x):
    return pltpu.roll(x, 64, 1)


def low_lanes(shape):
    return lax.broadcasted_iota(jnp.int32, shape, 1) < 64


def spread_kernel(
    t_shift, s_shift, tq, tk, tv, hidden, wq, wk, wv,
    keys, cols,
    near_a, near_b, near_s, stud, piece, transit, hid,
    a_send, a_recv, b_send, b_recv, s_send, s_recv,
    p_send, key_sem, tr_sem, f_send, g_send, r_send, h_send, h_recv,
):
    seq, head, y, z, x, c = place()
    sibling = (seq, head + 1 - 2 * c)
    behind = (seq, (head + 7) % 8)
    peers = [sibling]
    for dz in range(1, NZ):
        other = y * NZ + (z + dz) % NZ
        peers.append((other, head))
        peers.append((other, sibling[1]))
    for dy in range(1, NY):
        peers.append((((y + dy) % NY) * NZ + z, head))
    peers.append((seq, (head + 7 + 2 * c) % 8))
    wait_all = greet(peers)

    for kind, weight in enumerate((wq, wk, wv)):
        stud[:, kind * 128 : (kind + 1) * 128] = jnp.dot(
            hidden[...], weight[...], preferred_element_type=F32
        ).astype(BF16)
    wait_all()

    teachers = (tq, tk, tv)
    outs = []
    for kind in range(3):
        outs.append(remote(teachers[kind].at[:, 0:128], near_a.at[kind], a_send.at[kind], a_recv.at[kind], behind))
    out_s = remote(stud, near_s, s_send, s_recv, behind)
    for kind in range(3):
        outs.append(remote(teachers[kind].at[:, 128:384], near_b.at[kind], b_send.at[kind], b_recv.at[kind], behind))
    for copy in outs[:3]:
        copy.start()
    out_s.start()
    for copy in outs[3:]:
        copy.start()

    def one_hot(rows, columns, first):
        there = lax.broadcasted_iota(jnp.int32, (rows, columns), 0)
        here = lax.broadcasted_iota(jnp.int32, (rows, columns), 1)
        return jnp.where(there == here + first, jnp.float32(1.0), jnp.float32(0.0)).astype(BF16)

    pick_t = one_hot(512, 256, t_shift[0] - 128)
    pick_s = one_hot(256, 128, s_shift[0])
    own_pair = c == y // 2
    core = z % 2

    def send_piece(k, go):
        target = (y * NZ + k, 2 * x + core)
        mine = jnp.logical_and(z == k, core == c)
        away = jnp.logical_not(mine)

        @pl.when(jnp.logical_and(own_pair, away))
        def _():
            copy = remote(piece.at[k], keys.at[seq], p_send.at[k], key_sem.at[seq], target)
            copy.start() if go else copy.wait_send()

        @pl.when(jnp.logical_and(jnp.logical_not(own_pair), away))
        def _():
            copy = remote(piece.at[k], transit.at[z // 2], p_send.at[k], tr_sem.at[z // 2], target)
            copy.start() if go else copy.wait_send()

        if go:
            @pl.when(jnp.logical_and(own_pair, mine))
            def _():
                pltpu.make_async_copy(piece.at[k], keys.at[seq], key_sem.at[seq]).start()

            @pl.when(jnp.logical_and(jnp.logical_not(own_pair), mine))
            def _():
                pltpu.make_async_copy(piece.at[k], transit.at[z // 2], tr_sem.at[z // 2]).start()

    low = low_lanes((64, 128))
    for j in range(2):
        for kind in range(3):
            if j == 0:
                outs[kind].wait_recv()
                if kind == 0:
                    out_s.wait_recv()
                window = jnp.dot(
                    teachers[kind][:, 128:512], pick_t[0:384], preferred_element_type=F32
                ) + jnp.dot(near_a[kind], pick_t[384:512], preferred_element_type=F32)
            else:
                outs[3 + kind].wait_recv()
                window = (
                    jnp.dot(teachers[kind][:, 384:512], pick_t[0:128], preferred_element_type=F32)
                    + jnp.dot(near_a[kind], pick_t[128:256], preferred_element_type=F32)
                    + jnp.dot(near_b[kind], pick_t[256:512], preferred_element_type=F32)
                )
            at = slice(kind * 128, (kind + 1) * 128)
            small = jnp.dot(stud[:, at], pick_s[0:128], preferred_element_type=F32) + jnp.dot(
                near_s[:, at], pick_s[128:256], preferred_element_type=F32
            )
            k = kind * 2 + j
            piece[k, 0:128] = window[:, 0:128].astype(BF16)
            piece[k, 128:256] = window[:, 128:256].astype(BF16)
            if j == 0:
                packed = jnp.where(low, small[0:64], swap_halves(small[64:128]))
            else:
                packed = jnp.where(low, swap_halves(small[0:64]), small[64:128])
            piece[k, 256:320] = packed.astype(BF16)
            send_piece(k, True)

    for part in range(4):
        for block in range(4):
            hid[part, :, block * 128 : (block + 1) * 128] = hidden[
                :, block * 512 + part * 128 : block * 512 + part * 128 + 128
            ]

    active = z < PAIRS

    def key_copy(slot, send, device):
        return remote(keys.at[slot], keys.at[slot], send, key_sem.at[slot], device)

    partner = ((y + 1 - 2 * (y % 2)) * NZ + z, head)
    far_row = 2 * (1 - y // 2)

    def forwards(i):
        slot = y * NZ + 2 * i + c
        first = key_copy(slot, f_send.at[i], partner)
        relay = key_copy(slot, r_send.at[i], sibling)
        others = [
            remote(transit.at[i], keys.at[slot], g_send.at[2 * i + b], key_sem.at[slot], ((far_row + b) * NZ + z, head))
            for b in range(2)
        ]
        return first, relay, others

    @pl.when(active)
    def _():
        for i in range(4):
            first, relay, others = forwards(i)
            remote(transit.at[i], transit.at[i], g_send.at[2 * i], tr_sem.at[i], partner).wait_recv()
            for copy in others:
                copy.start()
            first.wait_recv()
            first.start()
            relay.start()

    columns_out = []
    for d in range(1, 4):
        to = (z + 2 * d) % NZ
        columns_out.append(
            remote(hid.at[to // 2], cols.at[z // 2], h_send.at[d], h_recv.at[z // 2], (y * NZ + to, head))
        )
    for copy in columns_out:
        copy.start()
    own_cols = pltpu.make_async_copy(hid.at[z // 2], cols.at[z // 2], h_recv.at[z // 2])
    own_cols.start()

    @pl.when(active)
    def _():
        for i in range(4):
            for n, dy in enumerate((1, 2, 3)):
                other = y // 2 * 2 + 1 - y % 2 if dy == 1 else far_row + dy - 2
                slot = other * NZ + 2 * i + c
                relay = key_copy(slot, r_send.at[4 + 3 * i + n], sibling)
                relay.wait_recv()
                relay.start()
        for i in range(4):
            for row in range(NY):
                slot = row * NZ + 2 * i + 1 - c
                key_copy(slot, r_send.at[0], sibling).wait_recv()
        for i in range(4):
            first, relay, others = forwards(i)
            first.wait_send()
            relay.wait_send()
            for copy in others:
                copy.wait_send()
            for n in range(3):
                key_copy(0, r_send.at[4 + 3 * i + n], sibling).wait_send()

    for part in range(4):
        pltpu.make_async_copy(hid.at[part], cols.at[part], h_recv.at[part]).wait()
    for copy in columns_out:
        copy.wait_send()
    for copy in outs:
        copy.wait_send()
    out_s.wait_send()
    for k in range(PAIRS):
        send_piece(k, False)


def spread(t_shift, s_shift, tq, tk, tv, hidden, wq, wk, wv):
    vmem = pl.BlockSpec(memory_space=pltpu.VMEM)
    smem = pl.BlockSpec(memory_space=pltpu.SMEM)
    dma = pltpu.SemaphoreType.DMA
    return pl.pallas_call(
        spread_kernel,
        name="spread",
        out_shape=(
            jax.ShapeDtypeStruct((SLOTS, PIECE, 128), BF16),
            jax.ShapeDtypeStruct((4, TOK, 512), BF16),
        ),
        in_specs=[smem, smem] + [vmem] * 7,
        out_specs=(pl.BlockSpec(memory_space=pl.ANY), pl.BlockSpec(memory_space=pl.ANY)),
        scratch_shapes=[
            pltpu.VMEM((3, TOK, 128), BF16),
            pltpu.VMEM((3, TOK, 256), BF16),
            pltpu.VMEM((TOK, 384), BF16),
            pltpu.VMEM((TOK, 384), BF16),
            pltpu.VMEM((PAIRS, PIECE, 128), BF16),
            pltpu.VMEM((4, PIECE, 128), BF16),
            pltpu.VMEM((4, TOK, 512), BF16),
            dma((3,)), dma((3,)), dma((3,)), dma((3,)), dma(()), dma(()),
            dma((PAIRS,)), dma((SLOTS,)), dma((4,)), dma((4,)), dma((8,)), dma((16,)), dma((4,)), dma((4,)),
        ],
        compiler_params=pltpu.CompilerParams(
            collective_id=0, has_side_effects=True, vmem_limit_bytes=32 * 1024 * 1024
        ),
    )(t_shift, s_shift, tq, tk, tv, hidden, wq, wk, wv)


def relate_kernel(where, lengths, keys, part, div, kt, ks, st, ss, acc, top_t, top_s, row_t, row_s, near):
    seq = where[0]
    c = where[1] % 2
    y = seq // NZ
    z = seq % NZ
    group = 2 * (y % 2) + c
    div[...] = jnp.zeros_like(div)
    coef = jnp.float32(1.0 / 48.0)
    scale_t = jnp.float32(1.0 / 16.0)
    scale_s = jnp.float32(1.0 / 8.0)
    sub = 32

    @pl.when(z < PAIRS)
    def _():
        low = low_lanes((64, 128))

        @pl.loop(0, SLOTS)
        def _(slot):
            base = pl.multiple_of(slot * TOK, TOK)
            kt[pl.ds(base, TOK), 0:128] = keys[slot, 0:128]
            kt[pl.ds(base, TOK), 128:256] = keys[slot, 128:256]
            packed = keys[slot, 256:320].astype(F32)
            zero = jnp.zeros_like(packed)
            ks[pl.ds(base, 64)] = jnp.where(low, packed, zero).astype(BF16)
            ks[pl.ds(base + 64, 64)] = jnp.where(low, swap_halves(packed), zero).astype(BF16)

        acc[...] = jnp.zeros_like(acc)
        end0 = lengths[0]
        end1 = end0 + lengths[1]
        end2 = end1 + lengths[2]

        def first_of(position):
            zero = jnp.int32(0)
            start = jnp.where(position >= end0, end0, zero)
            start = jnp.where(position >= end1, end1, start)
            return jnp.where(position >= end2, end2, start)

        @pl.loop(0, 4)
        def _(t):
            odd = t % 2
            block = 4 * t + odd * 3 + (1 - 2 * odd) * group
            r0 = pl.multiple_of(block * ROWS, ROWS)
            lower = first_of(r0) // CHUNK
            upper = (r0 + ROWS - 1) // CHUNK + 1
            top_t[...] = jnp.full_like(top_t, NEG)
            top_s[...] = jnp.full_like(top_s, NEG)

            @pl.loop(lower, upper)
            def _(n):
                k0 = pl.multiple_of(n * CHUNK, CHUNK)
                dims = (((1,), (1,)), ((), ()))
                st[:, pl.ds(k0, CHUNK)] = lax.dot_general(
                    kt[pl.ds(r0, ROWS)], kt[pl.ds(k0, CHUNK)], dims, preferred_element_type=F32
                )
                ss[:, pl.ds(k0, CHUNK)] = lax.dot_general(
                    ks[pl.ds(r0, ROWS)], ks[pl.ds(k0, CHUNK)], dims, preferred_element_type=F32
                )

                @pl.loop(0, ROWS // sub)
                def _(r):
                    at = pl.multiple_of(r * sub, sub)
                    row = r0 + at + lax.broadcasted_iota(jnp.int32, (sub, 128), 0)
                    start = first_of(row)
                    mt = top_t[pl.ds(at, sub)]
                    ms = top_s[pl.ds(at, sub)]
                    for q in range(CHUNK // 128):
                        c0 = pl.multiple_of(k0 + q * 128, 128)
                        column = c0 + lax.broadcasted_iota(jnp.int32, (sub, 128), 1)
                        allowed = jnp.logical_and(column >= start, column <= row)
                        a = jnp.where(allowed, st[pl.ds(at, sub), pl.ds(c0, 128)] * scale_t, NEG)
                        b = jnp.where(allowed, ss[pl.ds(at, sub), pl.ds(c0, 128)] * scale_s, NEG)
                        st[pl.ds(at, sub), pl.ds(c0, 128)] = a
                        ss[pl.ds(at, sub), pl.ds(c0, 128)] = b
                        mt = jnp.maximum(mt, a)
                        ms = jnp.maximum(ms, b)
                    top_t[pl.ds(at, sub)] = mt
                    top_s[pl.ds(at, sub)] = ms

            @pl.loop(0, ROWS // sub)
            def _(r):
                at = pl.multiple_of(r * sub, sub)
                mt = jnp.max(top_t[pl.ds(at, sub)], axis=1, keepdims=True)
                ms = jnp.max(top_s[pl.ds(at, sub)], axis=1, keepdims=True)
                zero = jnp.zeros((sub, 128), F32)

                def body(n, carry):
                    tot_t, tot_s, cross = carry
                    k0 = pl.multiple_of(n * CHUNK, CHUNK)
                    for q in range(CHUNK // 128):
                        c0 = pl.multiple_of(k0 + q * 128, 128)
                        a = st[pl.ds(at, sub), pl.ds(c0, 128)]
                        b = ss[pl.ds(at, sub), pl.ds(c0, 128)]
                        ea = jnp.exp(a - mt)
                        eb = jnp.exp(b - ms)
                        st[pl.ds(at, sub), pl.ds(c0, 128)] = ea
                        ss[pl.ds(at, sub), pl.ds(c0, 128)] = eb
                        tot_t = tot_t + ea
                        tot_s = tot_s + eb
                        cross = cross + ea * (a - b)
                    return tot_t, tot_s, cross

                tot_t, tot_s, cross = lax.fori_loop(lower, upper, body, (zero, zero, zero))
                tot_t = jnp.sum(tot_t, axis=1, keepdims=True)
                tot_s = jnp.sum(tot_s, axis=1, keepdims=True)
                cross = jnp.sum(cross, axis=1, keepdims=True)
                value = cross / tot_t + (ms + jnp.log(tot_s)) - (mt + jnp.log(tot_t))
                spread_value = jnp.broadcast_to(value * jnp.float32(1.0 / 128.0), (sub, 128))
                add = spread_value[0:8]
                for m in range(1, sub // 8):
                    add = add + spread_value[8 * m : 8 * m + 8]
                div[...] += add
                row_t[pl.ds(at, sub)] = jnp.broadcast_to(coef / tot_t, (sub, 128))
                row_s[pl.ds(at, sub)] = jnp.broadcast_to(coef / tot_s, (sub, 128))

            near[...] = jnp.zeros_like(near)

            @pl.loop(lower, upper)
            def _(n):
                k0 = pl.multiple_of(n * CHUNK, CHUNK)
                wide_t = jnp.concatenate([row_t[...]] * (CHUNK // 128), axis=1)
                wide_s = jnp.concatenate([row_s[...]] * (CHUNK // 128), axis=1)
                g = (ss[:, pl.ds(k0, CHUNK)] * wide_s - st[:, pl.ds(k0, CHUNK)] * wide_t).astype(BF16)
                near[...] += jnp.dot(g, ks[pl.ds(k0, CHUNK)], preferred_element_type=F32)
                acc[pl.ds(k0, CHUNK)] += lax.dot_general(
                    g, ks[pl.ds(r0, ROWS)], (((0,), (0,)), ((), ())), preferred_element_type=F32
                )

            acc[pl.ds(r0, ROWS)] += near[...]

        for row in range(NY):
            for parity in range(2):
                for i in range(4):
                    base = (row * NZ + 2 * i + parity) * TOK
                    part[row, parity, i] = (
                        jnp.where(low, acc[base : base + 64], swap_halves(acc[base + 64 : base + 128])) * scale_s
                    ).astype(BF16)


def relate(where, lengths, keys):
    vmem = pl.BlockSpec(memory_space=pltpu.VMEM)
    smem = pl.BlockSpec(memory_space=pltpu.SMEM)
    return pl.pallas_call(
        relate_kernel,
        name="relate",
        out_shape=(
            jax.ShapeDtypeStruct((NY, 2, 4, 64, 128), BF16),
            jax.ShapeDtypeStruct((8, 128), F32),
        ),
        in_specs=[smem, smem, vmem],
        out_specs=(vmem, vmem),
        scratch_shapes=[
            pltpu.VMEM((KEYS, 256), BF16),
            pltpu.VMEM((KEYS, 128), BF16),
            pltpu.VMEM((ROWS, KEYS), F32),
            pltpu.VMEM((ROWS, KEYS), F32),
            pltpu.VMEM((KEYS, 128), F32),
            pltpu.VMEM((ROWS, 128), F32),
            pltpu.VMEM((ROWS, 128), F32),
            pltpu.VMEM((ROWS, 128), F32),
            pltpu.VMEM((ROWS, 128), F32),
            pltpu.VMEM((ROWS, 128), F32),
        ],
        compiler_params=pltpu.CompilerParams(vmem_limit_bytes=40 * 1024 * 1024),
    )(where, lengths, keys)


def fold_kernel(
    s_shift, part, div, cols,
    mean, gq, gk, gv,
    in1, sums, in2, db, outp, in4, win, prev, div_a, div_b, div_c, div_1, div_2,
    s1, r1, s2, r2, s4, r4, sw, rw, sa, ra, sb, rb, sc, rc,
):
    seq, head, y, z, x, c = place()
    ahead = (seq, (head + 1) % 8)
    other = head + 1 - 2 * c
    peers = [(seq, (head + d) % 8) for d in range(1, 8)]
    for dz in range(1, NZ):
        for h in (head, other):
            peers.append((y * NZ + (z + dz) % NZ, h))
    for dy in range(1, NY):
        for h in (head, other):
            peers.append((((y + dy) % NY) * NZ + z, h))
        peers.append((((y + dy) % NY) * NZ + z + 1 - 2 * (z % 2), head))
    greet(peers)()
    active = z < PAIRS

    def row_copies():
        me = y * 2 + c
        copies = []
        for dy in range(1, NY):
            row = (y + dy) % NY
            for core in range(2):
                copies.append(
                    remote(part.at[row, core], in1.at[me], s1.at[2 * dy + core], r1.at[me], (row * NZ + z, 2 * x + core))
                )
        copies.append(remote(part.at[y, 1 - c], in1.at[me], s1.at[0], r1.at[me], (seq, other)))
        return copies

    own_div = pltpu.make_async_copy(div, div_a.at[y], ra.at[y])
    own_div.start()
    div_row = [
        remote(div, div_a.at[y], sa.at[dy], ra.at[y], (((y + dy) % NY) * NZ + z, head)) for dy in range(1, NY)
    ]

    @pl.when(active)
    def _():
        pltpu.make_async_copy(part.at[y, c], in1.at[y * 2 + c], r1.at[y * 2 + c]).start()
        for copy in row_copies():
            copy.start()

    for copy in div_row:
        copy.start()

    def pair_copies(p):
        copies = []
        for i in range(4):
            copies.append((i, remote(sums.at[p], in2.at[z], s2.at[p * 4 + i], r2.at[z], (y * NZ + 2 * i + c, 2 * x + p))))
        return copies

    def each_pair_copy(p, go):
        for i, copy in pair_copies(p):
            mine = jnp.logical_and(z == 2 * i + c, c == p)

            @pl.when(jnp.logical_not(mine))
            def _():
                copy.start() if go else copy.wait_send()

            if go:
                @pl.when(mine)
                def _():
                    pltpu.make_async_copy(sums.at[p], in2.at[z], r2.at[z]).start()

    @pl.when(active)
    def _():
        for p in range(2):
            total = jnp.zeros((4, 64, 128), F32)
            for n in range(4):
                pltpu.make_async_copy(in1.at[4 * p + n], in1.at[4 * p + n], r1.at[4 * p + n]).wait()
                total = total + in1[4 * p + n].astype(F32)
            sums[p] = total.astype(BF16)
            each_pair_copy(p, True)

    for n in range(NY):
        pltpu.make_async_copy(div_a.at[n], div_a.at[n], ra.at[n]).wait()
    div_1[...] = (div_a[0] + div_a[1]) + (div_a[2] + div_a[3])
    pltpu.make_async_copy(div_1, div_b.at[z], rb.at[z]).start()
    div_col = [
        remote(div_1, div_b.at[z], sb.at[dz], rb.at[z], (y * NZ + (z + dz) % NZ, head)) for dz in range(1, NZ)
    ]
    for copy in div_col:
        copy.start()

    def eight(buf):
        return ((buf[0] + buf[1]) + (buf[2] + buf[3])) + ((buf[4] + buf[5]) + (buf[6] + buf[7]))

    for n in range(NZ):
        pltpu.make_async_copy(div_b.at[n], div_b.at[n], rb.at[n]).wait()
    div_2[...] = eight(div_b)
    pltpu.make_async_copy(div_2, div_c.at[head], rc.at[head]).start()
    div_head = [
        remote(div_2, div_c.at[head], sc.at[d], rc.at[head], (seq, (head + d) % 8)) for d in range(1, 8)
    ]
    for copy in div_head:
        copy.start()

    low = low_lanes((64, 128))
    for kind in range(3):
        for j in range(2):
            k = 2 * kind + j
            pltpu.make_async_copy(in2.at[k], in2.at[k], r2.at[k]).wait()
        for i in range(4):
            p0 = in2[2 * kind, i].astype(F32)
            p1 = in2[2 * kind + 1, i].astype(F32)
            at = slice(kind * 128, (kind + 1) * 128)
            db[i * 128 : i * 128 + 64, at] = jnp.where(low, p0, swap_halves(p1)).astype(BF16)
            db[i * 128 + 64 : i * 128 + 128, at] = jnp.where(low, swap_halves(p0), p1).astype(BF16)
    grad = jnp.zeros((512, 384), F32)
    for i in range(4):
        grad = grad + lax.dot_general(
            cols[i], db[i * 128 : (i + 1) * 128], (((0,), (0,)), ((), ())), preferred_element_type=F32
        )
    for n in range(8):
        outp[n] = grad[n * 64 : (n + 1) * 64].astype(BF16)

    slot = y * 2 + z % 2
    pltpu.make_async_copy(outp.at[slot], in4.at[slot], r4.at[slot]).start()
    block_copies = []
    for d in range(1, 8):
        to = (slot + d) % 8
        block_copies.append(
            remote(
                outp.at[to], in4.at[slot], s4.at[d], r4.at[slot],
                ((to // 2) * NZ + (z // 2) * 2 + to % 2, head),
            )
        )
    for copy in block_copies:
        copy.start()
    total = jnp.zeros((64, 384), F32)
    for n in range(8):
        pltpu.make_async_copy(in4.at[n], in4.at[n], r4.at[n]).wait()
        total = total + in4[n].astype(F32)
    win[...] = total.astype(BF16)
    last = remote(win, prev, sw, rw, ahead)
    last.start()

    there = lax.broadcasted_iota(jnp.int32, (256, 128), 0)
    here = lax.broadcasted_iota(jnp.int32, (256, 128), 1)
    pick = jnp.where(there == here + (128 - s_shift[0]), jnp.float32(1.0), jnp.float32(0.0)).astype(BF16)
    for n in range(8):
        pltpu.make_async_copy(div_c.at[n], div_c.at[n], rc.at[n]).wait()
    mean[0, 0] = jnp.sum(eight(div_c)) * jnp.float32(1.0 / 196608.0)
    last.wait_recv()
    for kind, out in enumerate((gq, gk, gv)):
        at = slice(kind * 128, (kind + 1) * 128)
        out[...] = (
            jnp.dot(prev[:, at], pick[0:128], preferred_element_type=F32)
            + jnp.dot(win[:, at], pick[128:256], preferred_element_type=F32)
        ).astype(BF16)

    last.wait_send()
    for copy in block_copies + div_head + div_col + div_row:
        copy.wait_send()

    @pl.when(active)
    def _():
        for copy in row_copies():
            copy.wait_send()
        for p in range(2):
            each_pair_copy(p, False)


def fold(s_shift, part, div, cols):
    vmem = pl.BlockSpec(memory_space=pltpu.VMEM)
    smem = pl.BlockSpec(memory_space=pltpu.SMEM)
    dma = pltpu.SemaphoreType.DMA
    grad = jax.ShapeDtypeStruct((64, 128), BF16)
    return pl.pallas_call(
        fold_kernel,
        name="fold",
        out_shape=(jax.ShapeDtypeStruct((1, 1), F32), grad, grad, grad),
        in_specs=[smem, vmem, vmem, vmem],
        out_specs=(smem, vmem, vmem, vmem),
        scratch_shapes=[
            pltpu.VMEM((8, 4, 64, 128), BF16),
            pltpu.VMEM((2, 4, 64, 128), BF16),
            pltpu.VMEM((PAIRS, 4, 64, 128), BF16),
            pltpu.VMEM((512, 384), BF16),
            pltpu.VMEM((8, 64, 384), BF16),
            pltpu.VMEM((8, 64, 384), BF16),
            pltpu.VMEM((64, 384), BF16),
            pltpu.VMEM((64, 384), BF16),
            pltpu.VMEM((NY, 8, 128), F32),
            pltpu.VMEM((NZ, 8, 128), F32),
            pltpu.VMEM((8, 8, 128), F32),
            pltpu.VMEM((8, 128), F32),
            pltpu.VMEM((8, 128), F32),
            dma((8,)), dma((8,)), dma((8,)), dma((PAIRS,)), dma((8,)), dma((8,)), dma(()), dma(()),
            dma((NY,)), dma((NY,)), dma((NZ,)), dma((NZ,)), dma((8,)), dma((8,)),
        ],
        compiler_params=pltpu.CompilerParams(
            collective_id=1, has_side_effects=True, vmem_limit_bytes=32 * 1024 * 1024
        ),
    )(s_shift, part, div, cols)


def local(
    teacher_query, teacher_key, teacher_value, student_hidden, weight_query, weight_key, weight_value,
    teacher_shift, student_shift, segment_lengths,
):
    keys, cols = spread(
        teacher_shift, student_shift, teacher_query, teacher_key, teacher_value, student_hidden,
        weight_query, weight_key, weight_value,
    )
    where = jnp.stack([lax.axis_index("seq"), lax.axis_index("head")]).astype(jnp.int32)
    part, div = relate(where, segment_lengths, keys)
    mean, gq, gk, gv = fold(student_shift, part, div, cols)
    return mean[0, 0], gq, gk, gv


def solution(mesh):
    in_specs = (
        P("seq", "head"),
        P("seq", "head"),
        P("seq", "head"),
        P("seq", None),
        P(None, "head"),
        P(None, "head"),
        P(None, "head"),
        P(),
        P(),
        P(),
    )
    out_specs = (P(), P("seq", "head"), P("seq", "head"), P("seq", "head"))
    return jax.shard_map(local, mesh=mesh, in_specs=in_specs, out_specs=out_specs, check_vma=False)
```

```python
import functools
import math

import jax
import jax.numpy as jnp
from jax import lax
from jax.experimental import pallas as pl
from jax.experimental.pallas import tpu as pltpu
from jax.sharding import PartitionSpec as P

MESH = pl.DeviceIdType.MESH
NEG = -1e30
TOK = 128
NZ = 8
NY = 4
PAIRS = 6
VMEM_LIMIT = 60 * 1024 * 1024
SLOTS = NY * NZ
PIECE = 320
ROWS = 256
CHUNK = 256
SUB = 64
FLIGHT = 3
PART = 272
KEYS = SLOTS * TOK
F32 = jnp.float32
BF16 = jnp.bfloat16


def place():
    seq = lax.axis_index("seq")
    head = lax.axis_index("head")
    return seq, head, seq // NZ, seq % NZ, head // 2, head % 2


def greet(peers):
    barrier = pltpu.get_barrier_semaphore()
    for peer in peers:
        pl.semaphore_signal(barrier, inc=1, device_id=peer, device_id_type=MESH)
    return lambda: pl.semaphore_wait(barrier, len(peers))


def remote(src, dst, send, recv, device):
    return pltpu.make_async_remote_copy(
        src_ref=src, dst_ref=dst, send_sem=send, recv_sem=recv, device_id=device, device_id_type=MESH
    )


def spread_kernel(
    t_shift, s_shift, tq, tk, tv, hidden, wq, wk, wv,
    keys, cols,
    teach, tokens, weights, near_n, near_p, small_n, small_p, stud, piece, transit, hid,
    load, n_send, n_recv, p_send, p_recv,
    k_send, key_sem, tr_sem, f_send, g_send, r_send, z_send, z_recv, h_send, h_recv,
):
    seq, head, y, z, x, c = place()
    sibling = (seq, head + 1 - 2 * c)
    behind = (seq, (head + 7) % 8)
    teachers = (tq, tk, tv)
    loads = [pltpu.make_async_copy(hidden, tokens, load.at[0])]
    for kind, weight in enumerate((wq, wk, wv)):
        loads.append(pltpu.make_async_copy(weight, weights.at[kind], load.at[1 + kind]))
    for kind in range(3):
        loads.append(pltpu.make_async_copy(teachers[kind], teach.at[kind], load.at[4 + kind]))
    for copy in loads:
        copy.start()

    peers = [(seq, (head + d) % 8) for d in range(1, 8)]
    for dz in range(1, NZ):
        other = y * NZ + (z + dz) % NZ
        peers.append((other, head))
        peers.append((other, sibling[1]))
    for dy in range(1, NY):
        peers.append((((y + dy) % NY) * NZ + z, head))
    wait_all = greet(peers)

    loads[0].wait()
    for kind in range(3):
        loads[1 + kind].wait()
        stud[:, kind * 128 : (kind + 1) * 128] = jnp.dot(
            tokens[...], weights[kind], preferred_element_type=F32
        ).astype(BF16)
    wait_all()

    ahead = (seq, (head + 1) % 8)
    outs = []
    for kind in range(3):
        outs.append(remote(teachers[kind].at[:, 0:128], near_n.at[kind], n_send.at[kind], n_recv.at[kind], behind))
        outs.append(remote(teachers[kind].at[:, 384:512], near_p.at[kind], p_send.at[kind], p_recv.at[kind], ahead))
    outs.append(remote(stud, small_n, n_send.at[3], n_recv.at[3], behind))
    outs.append(remote(stud, small_p, p_send.at[3], p_recv.at[3], ahead))
    for copy in outs:
        copy.start()

    for part in range(4):
        first = pl.multiple_of(head // 2 * 512 + part * 128, 128)
        hid[part] = jnp.transpose(tokens[:, pl.ds(first, 128)].astype(F32)).astype(BF16)
    mine = pl.ds(pl.multiple_of(c * 64, 64), 64)
    column_outs = []
    for d in range(1, 4):
        to = (z + 2 * d) % NZ
        column_outs.append(
            remote(
                hid.at[to // 2, mine], cols.at[head, z // 2], z_send.at[d], z_recv.at[z // 2], (y * NZ + to, head)
            )
        )
    for copy in column_outs:
        copy.start()
    pltpu.make_async_copy(hid.at[z // 2, mine], cols.at[head, z // 2], z_recv.at[z // 2]).start()

    def one_hot(rows, columns, first, dim):
        there = lax.broadcasted_iota(jnp.int32, (rows, columns), dim)
        here = lax.broadcasted_iota(jnp.int32, (rows, columns), 1 - dim)
        return jnp.where(there == here + first, jnp.float32(1.0), jnp.float32(0.0)).astype(BF16)

    pick_t = one_hot(512, 256, t_shift[0] - 128, 0)
    pick_s = (one_hot(64, 256, s_shift[0] + 64, 1), one_hot(64, 256, s_shift[0], 1))
    own_pair = c == y // 2
    core = z % 2

    def send_piece(k, go):
        target = (y * NZ + k, 2 * x + core)
        some = k < PAIRS
        here = jnp.logical_and(some, jnp.logical_and(z == k, core == c))
        there = jnp.logical_and(some, jnp.logical_not(here))

        @pl.when(jnp.logical_and(own_pair, there))
        def _():
            copy = remote(piece.at[k], keys.at[seq], k_send.at[k], key_sem.at[seq], target)
            copy.start() if go else copy.wait_send()

        @pl.when(jnp.logical_and(jnp.logical_not(own_pair), there))
        def _():
            copy = remote(piece.at[k], transit.at[z // 2], k_send.at[k], tr_sem.at[z // 2], target)
            copy.start() if go else copy.wait_send()

        if go:
            @pl.when(jnp.logical_and(own_pair, here))
            def _():
                pltpu.make_async_copy(piece.at[k], keys.at[seq], key_sem.at[seq]).start()

            @pl.when(jnp.logical_and(jnp.logical_not(own_pair), here))
            def _():
                pltpu.make_async_copy(piece.at[k], transit.at[z // 2], tr_sem.at[z // 2]).start()

    transposed = (((1,), (1,)), ((), ()))
    for copy in loads[4:]:
        copy.wait()
    for copy in outs[6:]:
        copy.wait_recv()
    for kind in range(3):
        outs[2 * kind].wait_recv()
        outs[2 * kind + 1].wait_recv()
        at = slice(kind * 128, (kind + 1) * 128)
        for j in range(2):
            own = teach[kind, :, 0:384] if j == 0 else teach[kind, :, 128:512]
            if j == 0:
                window = jnp.dot(near_p[kind], pick_t[0:128], preferred_element_type=F32) + jnp.dot(
                    own, pick_t[128:512], preferred_element_type=F32
                )
                before, after = small_p[:, at], stud[:, at]
            else:
                window = jnp.dot(own, pick_t[0:384], preferred_element_type=F32) + jnp.dot(
                    near_n[kind], pick_t[384:512], preferred_element_type=F32
                )
                before, after = stud[:, at], small_n[:, at]
            small = lax.dot_general(
                pick_s[j][:, 0:128], before, transposed, preferred_element_type=F32
            ) + lax.dot_general(pick_s[j][:, 128:256], after, transposed, preferred_element_type=F32)
            k = kind * 2 + j
            piece[k, 0:128] = window[:, 0:128].astype(BF16)
            piece[k, 128:256] = window[:, 128:256].astype(BF16)
            piece[k, 256:320] = small.astype(BF16)
    order = [(z + d + NZ) % NZ for d in (0, 1, -1, 2, -2, 3, -3, 4)]
    for n, k in enumerate(order):
        if n > FLIGHT:
            send_piece(order[n - 1 - FLIGHT], False)
        send_piece(k, True)

    active = z < PAIRS

    def key_copy(slot, send, device):
        return remote(keys.at[slot], keys.at[slot], send, key_sem.at[slot], device)

    partner = ((y + 1 - 2 * (y % 2)) * NZ + z, head)
    far_row = 2 * (1 - y // 2)

    def forwards(i):
        slot = y * NZ + 2 * i + c
        first = key_copy(slot, f_send.at[i], partner)
        relay = key_copy(slot, r_send.at[i], sibling)
        others = [
            remote(transit.at[i], keys.at[slot], g_send.at[2 * i + b], key_sem.at[slot], ((far_row + b) * NZ + z, head))
            for b in range(2)
        ]
        return first, relay, others

    def arrival(turn):
        same = (0, 2, 6, 4)[turn]
        cross = (1, 7, 3, 5)[turn]
        return (z + jnp.where(core == c, same, cross)) % NZ // 2

    @pl.when(active)
    def _():
        for turn in range(4):
            i = arrival(turn)
            first, relay, others = forwards(i)
            remote(transit.at[i], transit.at[i], g_send.at[2 * i], tr_sem.at[i], partner).wait_recv()
            for copy in others:
                copy.start()
            first.wait_recv()
            first.start()
            relay.start()

    for i in range(4):
        pltpu.make_async_copy(hid.at[i, mine], cols.at[head, i], z_recv.at[i]).wait()
    head_outs = []
    for d in range(1, 8):
        head_outs.append(
            remote(cols.at[head], cols.at[head], h_send.at[d], h_recv.at[head], (seq, (head + d) % 8))
        )
    for copy in head_outs:
        copy.start()

    @pl.when(active)
    def _():
        for turn in range(4):
            i = arrival(turn)
            for n in range(3):
                other = y // 2 * 2 + 1 - y % 2 if n == 0 else far_row + n - 1
                slot = other * NZ + 2 * i + c
                relay = key_copy(slot, r_send.at[4 + 3 * turn + n], sibling)
                relay.wait_recv()
                relay.start()
        for i in range(4):
            for row in range(NY):
                slot = row * NZ + 2 * i + 1 - c
                key_copy(slot, r_send.at[0], sibling).wait_recv()
        for i in range(4):
            first, relay, others = forwards(i)
            first.wait_send()
            relay.wait_send()
            for copy in others:
                copy.wait_send()
            for n in range(3):
                key_copy(0, r_send.at[4 + 3 * i + n], sibling).wait_send()

    for d in range(1, 8):
        other = (head + d) % 8
        remote(cols.at[other], cols.at[other], h_send.at[d], h_recv.at[other], sibling).wait_recv()
    for copy in head_outs + column_outs + outs:
        copy.wait_send()
    for k in order[NZ - 1 - FLIGHT :]:
        send_piece(k, False)


def spread(t_shift, s_shift, tq, tk, tv, hidden, wq, wk, wv):
    anywhere = pl.BlockSpec(memory_space=pl.ANY)
    smem = pl.BlockSpec(memory_space=pltpu.SMEM)
    dma = pltpu.SemaphoreType.DMA
    return pl.pallas_call(
        spread_kernel,
        name="spread",
        out_shape=(
            jax.ShapeDtypeStruct((SLOTS, PIECE, 128), BF16),
            jax.ShapeDtypeStruct((8, 4, 64, TOK), BF16),
        ),
        in_specs=[smem, smem] + [anywhere] * 7,
        out_specs=(anywhere, anywhere),
        scratch_shapes=[
            pltpu.VMEM((3, TOK, 512), BF16),
            pltpu.VMEM((TOK, 2048), BF16),
            pltpu.VMEM((3, 2048, 128), BF16),
            pltpu.VMEM((3, TOK, 128), BF16),
            pltpu.VMEM((3, TOK, 128), BF16),
            pltpu.VMEM((TOK, 384), BF16),
            pltpu.VMEM((TOK, 384), BF16),
            pltpu.VMEM((TOK, 384), BF16),
            pltpu.VMEM((NZ, PIECE, 128), BF16),
            pltpu.VMEM((4, PIECE, 128), BF16),
            pltpu.VMEM((4, 128, TOK), BF16),
            dma((7,)), dma((4,)), dma((4,)), dma((4,)), dma((4,)),
            dma((NZ,)), dma((SLOTS,)), dma((4,)), dma((4,)), dma((8,)), dma((16,)),
            dma((4,)), dma((4,)), dma((8,)), dma((8,)),
        ],
        compiler_params=pltpu.CompilerParams(
            collective_id=0, has_side_effects=True, vmem_limit_bytes=VMEM_LIMIT
        ),
    )(t_shift, s_shift, tq, tk, tv, hidden, wq, wk, wv)


def in_three(row):
    high = row.astype(BF16).astype(F32)
    middle = (row - high).astype(BF16).astype(F32)
    low = row - high - middle
    at = lax.broadcasted_iota(jnp.int32, (16, 128), 0)
    tile = jnp.where(at == 0, high, jnp.where(at == 1, middle, jnp.where(at == 2, low, jnp.float32(0.0))))
    return tile.astype(BF16)


def relate_kernel(
    lengths, keys, part, div, kt, kst, st, ss, acc, top_t, top_s, row_t, row_s, cross, begin, load
):
    _, _, y, z, _, c = place()
    group = 2 * (y % 2) + c
    div[...] = jnp.zeros_like(div)
    coef = jnp.float32(1.0 / 48.0)
    scale = jnp.float32(1.0 / 16.0)
    scale2 = jnp.float32(math.log2(math.e) / 16.0)
    span = CHUNK // TOK
    blocks = KEYS // ROWS

    @pl.when(z < PAIRS)
    def _():
        loads = [
            pltpu.make_async_copy(keys.at[:, 0:128], kt.at[:, :, 0:128], load.at[0]),
            pltpu.make_async_copy(keys.at[:, 128:256], kt.at[:, :, 128:256], load.at[1]),
            pltpu.make_async_copy(keys.at[:, 256:320], kst, load.at[2]),
        ]
        for copy in loads:
            copy.start()
        acc[...] = jnp.zeros_like(acc)
        end0 = lengths[0]
        end1 = end0 + lengths[1]
        end2 = end1 + lengths[2]

        def first_of(position):
            zero = jnp.int32(0)
            start = jnp.where(position >= end0, end0, zero)
            start = jnp.where(position >= end1, end1, start)
            return jnp.where(position >= end2, end2, start)

        most = jnp.maximum(jnp.maximum(lengths[0], lengths[1]), jnp.maximum(lengths[2], lengths[3]))
        last = jnp.where(
            lengths[0] == most, end0, jnp.where(lengths[1] == most, end1, jnp.where(lengths[2] == most, end2, KEYS))
        )
        last_block = (last - 1) // ROWS
        for copy in loads:
            copy.wait()

        @pl.loop(0, 4)
        def _(t):
            odd = t % 2
            nth = 4 * t + odd * 3 + (1 - 2 * odd) * group
            block = (last_block + blocks - nth) % blocks
            r0 = block * ROWS
            lower = first_of(r0) // CHUNK
            upper = (r0 + ROWS - 1) // CHUNK + 1
            latest = first_of(r0 + ROWS - 1)
            top_t[...] = jnp.full_like(top_t, NEG)
            top_s[...] = jnp.full_like(top_s, NEG)
            begin[...] = first_of(r0 + lax.broadcasted_iota(jnp.int32, (ROWS, 128), 0))
            two = ROWS // TOK
            bt = jnp.concatenate([kst[block * two + u] for u in range(two)], axis=1)
            b2 = (jnp.transpose(bt.astype(F32)) * jnp.float32(2.0)).astype(BF16)

            def key_columns(n):
                return jnp.concatenate([kst[n * span + u] for u in range(span)], axis=1)

            def scores(n):
                a = lax.dot_general(
                    kt[pl.ds(block * two, two)].reshape(ROWS, 256),
                    kt[pl.ds(n * span, span)].reshape(CHUNK, 256),
                    (((1,), (1,)), ((), ())),
                    preferred_element_type=F32,
                )
                return a, jnp.dot(b2, key_columns(n), preferred_element_type=F32)

            def online(n, a, b, allowed):
                k0 = pl.multiple_of(n * CHUNK, CHUNK)
                for r in range(0, ROWS, SUB):
                    rows = slice(r, r + SUB)
                    xs = []
                    ws = []
                    for q in range(span):
                        x = a[rows, q * 128 : q * 128 + 128]
                        w = b[rows, q * 128 : q * 128 + 128]
                        if allowed is not None:
                            keep = allowed(k0 + q * 128, r)
                            x = jnp.where(keep, x, NEG)
                            w = jnp.where(keep, w, NEG)
                        at = pl.ds(pl.multiple_of(k0 + q * 128, 128), 128)
                        st[rows, at] = x
                        ss[rows, at] = w
                        xs.append(x)
                        ws.append(w)
                    old_t = top_t[rows]
                    old_s = top_s[rows]
                    mt = functools.reduce(jnp.maximum, xs, old_t)
                    ms = functools.reduce(jnp.maximum, ws, old_s)
                    top_t[rows] = mt
                    top_s[rows] = ms
                    fade = jnp.exp2((old_t - mt) * scale2)
                    tot_t = row_t[rows] * fade
                    mix = cross[rows] * fade
                    tot_s = row_s[rows] * jnp.exp2((old_s - ms) * scale2)
                    for x, w in zip(xs, ws):
                        ea = jnp.exp2((x - mt) * scale2)
                        tot_t = tot_t + ea
                        tot_s = tot_s + jnp.exp2((w - ms) * scale2)
                        mix = mix + ea * (x - w)
                    row_t[rows] = tot_t
                    row_s[rows] = tot_s
                    cross[rows] = mix

            def masked(n):
                def allowed(c0, r):
                    row = r0 + r + lax.broadcasted_iota(jnp.int32, (SUB, 128), 0)
                    column = c0 + lax.broadcasted_iota(jnp.int32, (SUB, 128), 1)
                    return jnp.logical_and(column >= begin[r : r + SUB], column <= row)

                online(n, *scores(n), allowed)

            def whole(n):
                online(n, *scores(n), None)

            row_t[...] = jnp.zeros_like(row_t)
            row_s[...] = jnp.zeros_like(row_s)
            cross[...] = jnp.zeros_like(cross)
            inner = jnp.minimum((latest + CHUNK - 1) // CHUNK, upper)
            outer = jnp.maximum((r0 + 1) // CHUNK, inner)

            @pl.loop(0, upper - lower - (outer - inner))
            def _(n):
                masked(jnp.where(lower + n < inner, lower + n, lower + n + (outer - inner)))

            @pl.loop(inner, outer)
            def _(n):
                whole(n)

            mt = jnp.max(top_t[...], axis=1, keepdims=True)
            ms = jnp.max(top_s[...], axis=1, keepdims=True)
            fade = jnp.exp2((top_t[...] - mt) * scale2)
            tot_t = jnp.sum(row_t[...] * fade, axis=1, keepdims=True)
            tot_s = jnp.sum(row_s[...] * jnp.exp2((top_s[...] - ms) * scale2), axis=1, keepdims=True)
            mixed = jnp.sum(cross[...] * fade, axis=1, keepdims=True)
            value = (mixed / tot_t + (ms - mt)) * scale + (jnp.log(tot_s) - jnp.log(tot_t))
            wide = jnp.broadcast_to(value * jnp.float32(1.0 / 128.0), (ROWS, 128))
            div[...] += jnp.sum(wide.reshape(ROWS // 8, 8, 128), axis=0)
            top_t[...] = jnp.broadcast_to(mt, (ROWS, 128))
            top_s[...] = jnp.broadcast_to(ms, (ROWS, 128))
            row_t[...] = jnp.broadcast_to(jnp.log2(coef / tot_t), (ROWS, 128))
            row_s[...] = jnp.broadcast_to(jnp.log2(coef / tot_s), (ROWS, 128))

            def gradient(n, near):
                k0 = pl.multiple_of(n * CHUNK, CHUNK)
                columns = []
                for q in range(span):
                    at = pl.ds(pl.multiple_of(k0 + q * 128, 128), 128)
                    columns.append(
                        (
                            jnp.exp2((ss[:, at] - top_s[...]) * scale2 + row_s[...])
                            - jnp.exp2((st[:, at] - top_t[...]) * scale2 + row_t[...])
                        ).astype(BF16)
                    )
                g = jnp.concatenate(columns, axis=1)
                acc[:, pl.ds(k0, CHUNK)] += jnp.dot(bt, g, preferred_element_type=F32)
                return near + lax.dot_general(
                    key_columns(n), g, (((1,), (1,)), ((), ())), preferred_element_type=F32
                )

            near = lax.fori_loop(lower, upper, gradient, jnp.zeros((64, ROWS), F32))
            acc[:, pl.ds(pl.multiple_of(r0, ROWS), ROWS)] += near

        tile = in_three(jnp.sum(div[...], axis=0, keepdims=True))
        for row in range(NY):
            for parity in range(2):
                for i in range(4):
                    base = (row * NZ + 2 * i + parity) * TOK
                    part[row, parity, i * 64 : (i + 1) * 64] = (
                        acc[:, base : base + TOK] * jnp.float32(1.0 / 8.0)
                    ).astype(BF16)
                part[row, parity, 256:PART] = tile


def relate(lengths, keys):
    vmem = pl.BlockSpec(memory_space=pltpu.VMEM)
    smem = pl.BlockSpec(memory_space=pltpu.SMEM)
    return pl.pallas_call(
        relate_kernel,
        name="relate",
        out_shape=(
            jax.ShapeDtypeStruct((NY, 2, PART, 128), BF16)
        ),
        in_specs=[smem, pl.BlockSpec(memory_space=pl.ANY)],
        out_specs=vmem,
        scratch_shapes=[
            pltpu.VMEM((8, 128), F32),
            pltpu.VMEM((SLOTS, TOK, 256), BF16),
            pltpu.VMEM((SLOTS, 64, TOK), BF16),
            pltpu.VMEM((ROWS, KEYS), F32),
            pltpu.VMEM((ROWS, KEYS), F32),
            pltpu.VMEM((64, KEYS), F32),
            pltpu.VMEM((ROWS, 128), F32),
            pltpu.VMEM((ROWS, 128), F32),
            pltpu.VMEM((ROWS, 128), F32),
            pltpu.VMEM((ROWS, 128), F32),
            pltpu.VMEM((ROWS, 128), F32),
            pltpu.VMEM((ROWS, 128), jnp.int32),
            pltpu.SemaphoreType.DMA((3,)),
        ],
        compiler_params=pltpu.CompilerParams(vmem_limit_bytes=VMEM_LIMIT),
    )(lengths, keys)


def fold_kernel(
    part, cols, mean, both,
    in1, sums, in2, outp, in4, win, prev, follow, div_x, div_1, fetched,
    load, s1, r1, s2, r2, s4, r4, sw, rw, sv, rv, sx, rx,
):
    seq, head, y, z, x, c = place()
    ahead = (seq, (head + 1) % 8)
    behind = (seq, (head + 7) % 8)
    other = head + 1 - 2 * c
    fetch = pltpu.make_async_copy(cols, fetched, load)
    fetch.start()
    peers = [(seq, (head + d) % 8) for d in range(1, 8)]
    for dz in range(1, NZ):
        for h in (head, other):
            peers.append((y * NZ + (z + dz) % NZ, h))
    for dy in range(1, NY):
        for h in (head, other):
            peers.append((((y + dy) % NY) * NZ + z, h))
        peers.append((((y + dy) % NY) * NZ + z + 1 - 2 * (z % 2), head))
    greet(peers)()
    active = z < PAIRS

    def row_copies():
        me = y * 2 + c
        copies = []
        for dy in (2, 1, 3):
            row = (y + dy) % NY
            for core in range(2):
                copies.append(
                    remote(part.at[row, core], in1.at[me], s1.at[2 * dy + core], r1.at[me], (row * NZ + z, 2 * x + core))
                )
        copies.append(remote(part.at[y, 1 - c], in1.at[me], s1.at[0], r1.at[me], (seq, other)))
        return copies

    @pl.when(active)
    def _():
        for copy in row_copies():
            copy.start()
        pltpu.make_async_copy(part.at[y, c], in1.at[y * 2 + c], r1.at[y * 2 + c]).start()

    def each_pair_copy(p, go):
        for i in range(4):
            copy = remote(sums.at[p], in2.at[z], s2.at[p * 4 + i], r2.at[z], (y * NZ + 2 * i + c, 2 * x + p))
            mine = jnp.logical_and(z == 2 * i + c, c == p)

            @pl.when(jnp.logical_not(mine))
            def _():
                copy.start() if go else copy.wait_send()

            if go:
                @pl.when(mine)
                def _():
                    pltpu.make_async_copy(sums.at[p], in2.at[z], r2.at[z]).start()

    @pl.when(active)
    def _():
        for p in range(2):
            total = jnp.zeros((256, 128), F32)
            tiles = jnp.zeros((16, 128), F32)
            for n in range(4 * p, 4 * p + 4):
                pltpu.make_async_copy(in1.at[n], in1.at[n], r1.at[n]).wait()
                total = total + in1[n, 0:256].astype(F32)
                tiles = tiles + in1[n, 256:PART].astype(F32)
            sums[p, 0:256] = total.astype(BF16)
            sums[p, 256:PART] = in_three(jnp.sum(tiles, axis=0, keepdims=True))
            each_pair_copy(p, True)

    fetch.wait()
    tiles = jnp.zeros((16, 128), F32)
    for k in range(PAIRS):
        pltpu.make_async_copy(in2.at[k], in2.at[k], r2.at[k]).wait()
        tiles = tiles + in2[k, 256:PART].astype(F32)
    grad = jnp.zeros((512, 384), F32)
    for i in range(4):
        grad = grad + lax.dot_general(
            fetched[:, i].reshape(512, TOK), in2[:, i * 64 : (i + 1) * 64].reshape(384, TOK),
            (((1,), (1,)), ((), ())),
            preferred_element_type=F32,
        )
    for n in range(8):
        outp[n] = grad[n * 64 : (n + 1) * 64].astype(BF16)

    slot = y * 2 + z % 2
    block_copies = []
    for d in (4, 5, 2, 3, 6, 7, 1):
        to = (slot + d) % 8
        block_copies.append(
            remote(
                outp.at[to], in4.at[slot], s4.at[d], r4.at[slot],
                ((to // 2) * NZ + (z // 2) * 2 + to % 2, head),
            )
        )
    for copy in block_copies:
        copy.start()
    pltpu.make_async_copy(outp.at[slot], in4.at[slot], r4.at[slot]).start()

    div_1[...] = jnp.broadcast_to(jnp.sum(tiles, axis=0, keepdims=True), (8, 128))
    pltpu.make_async_copy(div_1, div_x.at[head], rx.at[head]).start()
    div_copies = [remote(div_1, div_x.at[head], sx.at[d], rx.at[head], (seq, (head + d) % 8)) for d in range(1, 8)]
    for copy in div_copies:
        copy.start()

    total = jnp.zeros((64, 384), F32)
    for n in range(8):
        pltpu.make_async_copy(in4.at[n], in4.at[n], r4.at[n]).wait()
        total = total + in4[n].astype(F32)
    win[...] = total.astype(BF16)
    lasts = [remote(win, prev, sw, rw, ahead), remote(win, follow, sv, rv, behind)]
    for copy in lasts:
        copy.start()
    both[:, 384:768] = win[...]
    for copy in block_copies + div_copies:
        copy.wait_send()

    @pl.when(active)
    def _():
        for copy in row_copies():
            copy.wait_send()
        for p in range(2):
            each_pair_copy(p, False)

    total = jnp.zeros((8, 128), F32)
    for n in range(8):
        pltpu.make_async_copy(div_x.at[n], div_x.at[n], rx.at[n]).wait()
        total = total + div_x[n]
    mean[0, 0] = jnp.sum(total[0:1]) * jnp.float32(1.0 / 196608.0)
    for copy in lasts:
        copy.wait_send()
        copy.wait_recv()
    both[:, 0:384] = prev[...]
    both[:, 768:1152] = follow[...]


def fold(part, cols):
    vmem = pl.BlockSpec(memory_space=pltpu.VMEM)
    smem = pl.BlockSpec(memory_space=pltpu.SMEM)
    dma = pltpu.SemaphoreType.DMA
    return pl.pallas_call(
        fold_kernel,
        name="fold",
        out_shape=(jax.ShapeDtypeStruct((1, 1), F32), jax.ShapeDtypeStruct((64, 1152), BF16)),
        in_specs=[pl.BlockSpec(memory_space=pl.ANY)] * 2,
        out_specs=(smem, vmem),
        scratch_shapes=[
            pltpu.VMEM((8, PART, 128), BF16),
            pltpu.VMEM((2, PART, 128), BF16),
            pltpu.VMEM((PAIRS, PART, 128), BF16),
            pltpu.VMEM((8, 64, 384), BF16),
            pltpu.VMEM((8, 64, 384), BF16),
            pltpu.VMEM((64, 384), BF16),
            pltpu.VMEM((64, 384), BF16),
            pltpu.VMEM((64, 384), BF16),
            pltpu.VMEM((8, 8, 128), F32),
            pltpu.VMEM((8, 128), F32),
            pltpu.VMEM((8, 4, 64, TOK), BF16),
            dma(()), dma((8,)), dma((8,)), dma((8,)), dma((PAIRS,)), dma((8,)), dma((8,)),
            dma(()), dma(()), dma(()), dma(()), dma((8,)), dma((8,)),
        ],
        compiler_params=pltpu.CompilerParams(
            collective_id=1, has_side_effects=True, vmem_limit_bytes=VMEM_LIMIT
        ),
    )(part, cols)


def shift_kernel(s_shift, both, gq, gk, gv):
    there = lax.broadcasted_iota(jnp.int32, (384, 128), 0)
    here = lax.broadcasted_iota(jnp.int32, (384, 128), 1)
    pick = jnp.where(there == here + (192 - s_shift[0]), jnp.float32(1.0), jnp.float32(0.0)).astype(BF16)
    for kind, out in enumerate((gq, gk, gv)):
        out[...] = functools.reduce(
            jnp.add,
            [
                jnp.dot(
                    both[:, 384 * n + 128 * kind : 384 * n + 128 * kind + 128],
                    pick[128 * n : 128 * n + 128],
                    preferred_element_type=F32,
                )
                for n in range(3)
            ],
        ).astype(BF16)


def shift(s_shift, both):
    vmem = pl.BlockSpec(memory_space=pltpu.VMEM)
    grad = jax.ShapeDtypeStruct((64, 128), BF16)
    return pl.pallas_call(
        shift_kernel,
        name="shift",
        out_shape=(grad, grad, grad),
        in_specs=[pl.BlockSpec(memory_space=pltpu.SMEM), vmem],
        out_specs=(vmem, vmem, vmem),
    )(s_shift, both)


def local(
    teacher_query, teacher_key, teacher_value, student_hidden, weight_query, weight_key, weight_value,
    teacher_shift, student_shift, segment_lengths,
):
    keys, cols = spread(
        teacher_shift, student_shift, teacher_query, teacher_key, teacher_value, student_hidden,
        weight_query, weight_key, weight_value,
    )
    mean, both = fold(relate(segment_lengths, keys), cols)
    return (mean[0, 0], *shift(student_shift, both))


def solution(mesh):
    in_specs = (
        P("seq", "head"),
        P("seq", "head"),
        P("seq", "head"),
        P("seq", None),
        P(None, "head"),
        P(None, "head"),
        P(None, "head"),
        P(),
        P(),
        P(),
    )
    out_specs = (P(), P("seq", "head"), P("seq", "head"), P("seq", "head"))
    return jax.shard_map(local, mesh=mesh, in_specs=in_specs, out_specs=out_specs, check_vma=False)
```

```python
import functools
import math

import jax
import jax.numpy as jnp
from jax import lax
from jax.experimental import pallas as pl
from jax.experimental.pallas import tpu as pltpu
from jax.sharding import PartitionSpec as P

MESH = pl.DeviceIdType.MESH
NEG = -1e30
TOK = 128
NZ = 8
NY = 4
PAIRS = 6
VMEM_LIMIT = 60 * 1024 * 1024
SLOTS = NY * NZ
PIECE = 320
ROWS = 256
CHUNK = 512
FLIGHT = 2
PART = 272
KEYS = SLOTS * TOK
F32 = jnp.float32
BF16 = jnp.bfloat16


def place():
    seq = lax.axis_index("seq")
    head = lax.axis_index("head")
    return seq, head, seq // NZ, seq % NZ, head // 2, head % 2


def pair_at(z, group):
    return (z + 4 * group) % NZ


def greet(peers):
    barrier = pltpu.get_barrier_semaphore()
    for peer in peers:
        pl.semaphore_signal(barrier, inc=1, device_id=peer, device_id_type=MESH)
    return lambda: pl.semaphore_wait(barrier, len(peers))


def remote(src, dst, send, recv, device):
    return pltpu.make_async_remote_copy(
        src_ref=src, dst_ref=dst, send_sem=send, recv_sem=recv, device_id=device, device_id_type=MESH
    )


def spread_kernel(
    t_shift, s_shift, tq, tk, tv, hidden, wq, wk, wv,
    keys, cols,
    stack, tokens, weights, small_n, small_p, stud, piece, transit, hid,
    load, n_send, n_recv, p_send, p_recv,
    k_send, key_sem, tr_sem, f_send, g_send, r_send, z_send, z_recv, h_send, h_recv,
):
    seq, head, y, z, x, c = place()
    sibling = (seq, head + 1 - 2 * c)
    behind = (seq, (head + 7) % 8)
    teachers = (tq, tk, tv)
    loads = [pltpu.make_async_copy(hidden, tokens, load.at[0])]
    for kind, weight in enumerate((wq, wk, wv)):
        loads.append(pltpu.make_async_copy(weight, weights.at[kind], load.at[1 + kind]))
    for kind in range(3):
        for j in range(2):
            loads.append(
                pltpu.make_async_copy(
                    teachers[kind].at[:, 128 * j : 128 * j + 384],
                    stack.at[2 * kind + j, :, 128 - 128 * j : 512 - 128 * j],
                    load.at[4 + 2 * kind + j],
                )
            )
    for copy in loads:
        copy.start()

    peers = [(seq, (head + d) % 8) for d in range(1, 8)]
    for dz in range(1, NZ):
        other = y * NZ + (z + dz) % NZ
        peers.append((other, head))
        peers.append((other, sibling[1]))
    for dy in range(1, NY):
        peers.append((((y + dy) % NY) * NZ + z, head))
    wait_all = greet(peers)

    loads[0].wait()
    for kind in range(3):
        loads[1 + kind].wait()
        stud[:, kind * 128 : (kind + 1) * 128] = jnp.dot(
            tokens[...], weights[kind], preferred_element_type=F32
        ).astype(BF16)
    wait_all()

    ahead = (seq, (head + 1) % 8)
    outs = []
    for kind in range(3):
        first, last = teachers[kind].at[:, 0:128], teachers[kind].at[:, 384:512]
        outs.append(
            remote(first, stack.at[2 * kind + 1, :, 384:512], n_send.at[kind], n_recv.at[kind], behind)
        )
        outs.append(remote(last, stack.at[2 * kind, :, 0:128], p_send.at[kind], p_recv.at[kind], ahead))
    outs.append(remote(stud, small_n, n_send.at[3], n_recv.at[3], behind))
    outs.append(remote(stud, small_p, p_send.at[3], p_recv.at[3], ahead))
    for copy in outs:
        copy.start()

    for part in range(4):
        first = pl.multiple_of(head // 2 * 512 + part * 128, 128)
        hid[part] = jnp.transpose(tokens[:, pl.ds(first, 128)].astype(F32)).astype(BF16)
    mine = pl.ds(pl.multiple_of(c * 64, 64), 64)
    column_outs = []
    for d in range(1, 4):
        to = (z + 2 * d) % NZ
        column_outs.append(
            remote(
                hid.at[to // 2, mine], cols.at[head, z // 2], z_send.at[d], z_recv.at[z // 2], (y * NZ + to, head)
            )
        )
    for copy in column_outs:
        copy.start()
    pltpu.make_async_copy(hid.at[z // 2, mine], cols.at[head, z // 2], z_recv.at[z // 2]).start()

    def one_hot(rows, columns, first, dim):
        there = lax.broadcasted_iota(jnp.int32, (rows, columns), dim)
        here = lax.broadcasted_iota(jnp.int32, (rows, columns), 1 - dim)
        return jnp.where(there == here + first, jnp.float32(1.0), jnp.float32(0.0)).astype(BF16)

    pick_t = one_hot(512, 256, t_shift[0] - 128, 0)
    pick_s = (one_hot(64, 256, s_shift[0] + 64, 1), one_hot(64, 256, s_shift[0], 1))
    own_pair = c == y // 2
    core = z % 2

    def send_piece(to, go):
        k = pair_at(to, c)
        target = (y * NZ + to, 2 * x + core)
        some = k < PAIRS
        here = jnp.logical_and(some, jnp.logical_and(z == to, core == c))
        there = jnp.logical_and(some, jnp.logical_not(here))

        @pl.when(jnp.logical_and(own_pair, there))
        def _():
            copy = remote(piece.at[k], keys.at[seq], k_send.at[k], key_sem.at[seq], target)
            copy.start() if go else copy.wait_send()

        @pl.when(jnp.logical_and(jnp.logical_not(own_pair), there))
        def _():
            copy = remote(piece.at[k], transit.at[z // 2], k_send.at[k], tr_sem.at[z // 2], target)
            copy.start() if go else copy.wait_send()

        if go:
            @pl.when(jnp.logical_and(own_pair, here))
            def _():
                pltpu.make_async_copy(piece.at[k], keys.at[seq], key_sem.at[seq]).start()

            @pl.when(jnp.logical_and(jnp.logical_not(own_pair), here))
            def _():
                pltpu.make_async_copy(piece.at[k], transit.at[z // 2], tr_sem.at[z // 2]).start()

    transposed = (((1,), (1,)), ((), ()))
    for copy in loads[4:]:
        copy.wait()
    for copy in outs[:6]:
        copy.wait_recv()
    window = jnp.dot(stack[...].reshape(PAIRS * TOK, 512), pick_t, preferred_element_type=F32)
    for k in range(PAIRS):
        piece[k, 0:128] = window[k * TOK : (k + 1) * TOK, 0:128].astype(BF16)
        piece[k, 128:256] = window[k * TOK : (k + 1) * TOK, 128:256].astype(BF16)
    for copy in outs[6:]:
        copy.wait_recv()
    for k in range(PAIRS):
        at = slice(k // 2 * 128, (k // 2 + 1) * 128)
        before, after = (small_p, stud) if k % 2 == 0 else (stud, small_n)
        pick = pick_s[k % 2]
        small = lax.dot_general(
            pick[:, 0:128], before[:, at], transposed, preferred_element_type=F32
        ) + lax.dot_general(pick[:, 128:256], after[:, at], transposed, preferred_element_type=F32)
        piece[k, 256:320] = small.astype(BF16)
    order = [(z + d + NZ) % NZ for d in (0, 1, -1, 2, -2, 3, -3, 4)]
    for n, to in enumerate(order):
        if n > FLIGHT:
            send_piece(order[n - 1 - FLIGHT], False)
        send_piece(to, True)

    active = pair_at(z, y // 2) < PAIRS
    passing = pair_at(z, 1 - y // 2) < PAIRS
    beside = y + 1 - 2 * (y % 2)
    partner = (beside * NZ + z, head)
    opposite = ((3 - y) * NZ + z, head)

    def key_copy(slot, send, device):
        return remote(keys.at[slot], keys.at[slot], send, key_sem.at[slot], device)

    def source(turn):
        same = (0, 2, 6, 4)[turn]
        cross = (1, 7, 3, 5)[turn]
        return (z + jnp.where(core == c, same, cross)) % NZ

    def forwards(turn):
        slot = y * NZ + source(turn)
        return key_copy(slot, f_send.at[turn], partner), key_copy(slot, r_send.at[turn], sibling)

    def passed(turn):
        slot = y * NZ + source(turn)
        i = source(turn) // 2
        return i, [
            remote(
                transit.at[i], keys.at[slot], g_send.at[2 * turn + n], key_sem.at[slot],
                ((row * NZ) + z, head),
            )
            for n, row in enumerate((3 - y, 3 - beside))
        ]

    for turn in range(4):
        @pl.when(passing)
        def _():
            i, copies = passed(turn)
            remote(transit.at[i], transit.at[i], g_send.at[2 * turn], tr_sem.at[i], partner).wait_recv()
            for copy in copies:
                copy.start()

        @pl.when(active)
        def _():
            first, relay = forwards(turn)
            first.wait_recv()
            first.start()
            relay.start()

    for i in range(4):
        pltpu.make_async_copy(hid.at[i, mine], cols.at[head, i], z_recv.at[i]).wait()
    head_outs = []
    for d in range(1, 8):
        head_outs.append(
            remote(cols.at[head], cols.at[head], h_send.at[d], h_recv.at[head], (seq, (head + d) % 8))
        )
    for copy in head_outs:
        copy.start()

    @pl.when(active)
    def _():
        for turn in range(4):
            for n, row in enumerate((beside, 3 - y, 3 - beside)):
                relay = key_copy(row * NZ + source(turn), r_send.at[4 + 3 * turn + n], sibling)
                relay.wait_recv()
                relay.start()
        for i in range(4):
            for row in range(NY):
                key_copy(row * NZ + 2 * i + 1 - c, r_send.at[0], sibling).wait_recv()
        for turn in range(4):
            key_copy(0, f_send.at[turn], partner).wait_send()
        for n in range(16):
            key_copy(0, r_send.at[n], sibling).wait_send()

    @pl.when(passing)
    def _():
        for turn in range(4):
            for copy in passed(turn)[1]:
                copy.wait_send()

    for d in range(1, 8):
        other = (head + d) % 8
        remote(cols.at[other], cols.at[other], h_send.at[d], h_recv.at[other], sibling).wait_recv()
    for copy in head_outs + column_outs + outs:
        copy.wait_send()
    for to in order[NZ - 1 - FLIGHT :]:
        send_piece(to, False)


def spread(t_shift, s_shift, tq, tk, tv, hidden, wq, wk, wv):
    anywhere = pl.BlockSpec(memory_space=pl.ANY)
    smem = pl.BlockSpec(memory_space=pltpu.SMEM)
    dma = pltpu.SemaphoreType.DMA
    return pl.pallas_call(
        spread_kernel,
        name="spread",
        out_shape=(
            jax.ShapeDtypeStruct((SLOTS, PIECE, 128), BF16),
            jax.ShapeDtypeStruct((8, 4, 64, TOK), BF16),
        ),
        in_specs=[smem, smem] + [anywhere] * 7,
        out_specs=(anywhere, anywhere),
        scratch_shapes=[
            pltpu.VMEM((PAIRS, TOK, 512), BF16),
            pltpu.VMEM((TOK, 2048), BF16),
            pltpu.VMEM((3, 2048, 128), BF16),
            pltpu.VMEM((TOK, 384), BF16),
            pltpu.VMEM((TOK, 384), BF16),
            pltpu.VMEM((TOK, 384), BF16),
            pltpu.VMEM((NZ, PIECE, 128), BF16),
            pltpu.VMEM((4, PIECE, 128), BF16),
            pltpu.VMEM((4, 128, TOK), BF16),
            dma((10,)), dma((4,)), dma((4,)), dma((4,)), dma((4,)),
            dma((NZ,)), dma((SLOTS,)), dma((4,)), dma((4,)), dma((8,)), dma((16,)),
            dma((4,)), dma((4,)), dma((8,)), dma((8,)),
        ],
        compiler_params=pltpu.CompilerParams(
            collective_id=0, has_side_effects=True, vmem_limit_bytes=VMEM_LIMIT
        ),
    )(t_shift, s_shift, tq, tk, tv, hidden, wq, wk, wv)


def in_three(row):
    high = row.astype(BF16).astype(F32)
    middle = (row - high).astype(BF16).astype(F32)
    low = row - high - middle
    at = lax.broadcasted_iota(jnp.int32, (16, 128), 0)
    tile = jnp.where(at == 0, high, jnp.where(at == 1, middle, jnp.where(at == 2, low, jnp.float32(0.0))))
    return tile.astype(BF16)


def relate_kernel(lengths, keys, part, kt, kst, ks, st, ss, acc, load):
    _, _, y, z, _, c = place()
    group = 2 * (y % 2) + c
    coef = jnp.float32(1.0 / 48.0)
    scale = jnp.float32(1.0 / 16.0)
    scale2 = jnp.float32(math.log2(math.e) / 16.0)
    span = CHUNK // TOK
    two = ROWS // TOK
    blocks = KEYS // ROWS
    last_dims = (((1,), (1,)), ((), ()))

    @pl.when(pair_at(z, y // 2) < PAIRS)
    def _():
        loads = [
            pltpu.make_async_copy(keys.at[:, 256:320], kst, load.at[2]),
            pltpu.make_async_copy(keys.at[:, 0:128], kt.at[:, :, 0:128], load.at[0]),
            pltpu.make_async_copy(keys.at[:, 128:256], kt.at[:, :, 128:256], load.at[1]),
        ]
        for copy in loads:
            copy.start()
        acc[...] = jnp.zeros_like(acc)
        end0 = lengths[0]
        end1 = end0 + lengths[1]
        end2 = end1 + lengths[2]

        def first_of(position):
            zero = jnp.int32(0)
            start = jnp.where(position >= end0, end0, zero)
            start = jnp.where(position >= end1, end1, start)
            return jnp.where(position >= end2, end2, start)

        most = jnp.maximum(jnp.maximum(lengths[0], lengths[1]), jnp.maximum(lengths[2], lengths[3]))
        last = jnp.where(
            lengths[0] == most, end0, jnp.where(lengths[1] == most, end1, jnp.where(lengths[2] == most, end2, KEYS))
        )
        last_block = (last - 1) // ROWS
        unit = jnp.where(
            lax.broadcasted_iota(jnp.int32, (TOK, TOK), 0) == lax.broadcasted_iota(jnp.int32, (TOK, TOK), 1),
            jnp.float32(1.0),
            jnp.float32(0.0),
        ).astype(BF16)
        loads[0].wait()

        @pl.loop(0, SLOTS // 4)
        def _(n):
            for u in range(4):
                ks[4 * n + u] = lax.dot_general(
                    unit, kst[4 * n + u], last_dims, preferred_element_type=F32
                ).astype(BF16)

        for copy in loads[1:]:
            copy.wait()

        def one_block(t, div):
            odd = t % 2
            nth = 4 * t + odd * 3 + (1 - 2 * odd) * group
            block = (last_block + blocks - nth) % blocks
            r0 = block * ROWS
            lower = first_of(r0) // CHUNK
            upper = (r0 + ROWS - 1) // CHUNK + 1
            latest = first_of(r0 + ROWS - 1)
            row = r0 + lax.broadcasted_iota(jnp.int32, (8, ROWS), 1)
            start = first_of(row)
            sub_row = lax.broadcasted_iota(jnp.int32, (8, ROWS), 0)
            bt = jnp.concatenate([kst[block * two + u] for u in range(two)], axis=1)
            b2 = (bt.astype(F32) * jnp.float32(2.0)).astype(BF16)

            def online(n, carry, mask):
                mt, ms, tot_t, tot_s, cross = carry
                k0 = pl.multiple_of(n * CHUNK, CHUNK)
                a = lax.dot_general(
                    kt[pl.ds(n * span, span)].reshape(CHUNK, 256),
                    kt[pl.ds(block * two, two)].reshape(ROWS, 256),
                    last_dims,
                    preferred_element_type=F32,
                )
                b = jnp.dot(ks[pl.ds(n * span, span)].reshape(CHUNK, 64), b2, preferred_element_type=F32)
                for first in range(0, CHUNK, 64):
                    xs, ws = [], []
                    new_t, new_s = mt, ms
                    for g in range(first, first + 64, 8):
                        x = a[g : g + 8]
                        w = b[g : g + 8]
                        if mask:
                            column = sub_row + (k0 + g)
                            allowed = jnp.logical_and(column >= start, column <= row)
                            x = jnp.where(allowed, x, NEG)
                            w = jnp.where(allowed, w, NEG)
                        st[pl.ds(pl.multiple_of(k0 + g, 8), 8)] = x
                        ss[pl.ds(pl.multiple_of(k0 + g, 8), 8)] = w
                        new_t = jnp.maximum(new_t, x)
                        new_s = jnp.maximum(new_s, w)
                        xs.append(x)
                        ws.append(w)
                    fade = jnp.exp2((mt - new_t) * scale2)
                    tot_t = tot_t * fade
                    cross = cross * fade
                    tot_s = tot_s * jnp.exp2((ms - new_s) * scale2)
                    mt, ms = new_t, new_s
                    for x, w in zip(xs, ws):
                        ea = jnp.exp2((x - mt) * scale2)
                        tot_t = tot_t + ea
                        tot_s = tot_s + jnp.exp2((w - ms) * scale2)
                        cross = cross + ea * (x - w)
                return mt, ms, tot_t, tot_s, cross

            inner = jnp.minimum((latest + CHUNK - 1) // CHUNK, upper)
            outer = jnp.maximum((r0 + 1) // CHUNK, inner)
            low = jnp.full((8, ROWS), NEG, F32)
            zero = jnp.zeros((8, ROWS), F32)
            carry = lax.fori_loop(
                0,
                upper - lower - (outer - inner),
                lambda n, carry: online(
                    jnp.where(lower + n < inner, lower + n, lower + n + (outer - inner)), carry, True
                ),
                (low, low, zero, zero, zero),
            )
            mt, ms, tot_t, tot_s, cross = lax.fori_loop(
                inner, outer, lambda n, carry: online(n, carry, False), carry
            )
            top_t = jnp.max(mt, axis=0, keepdims=True)
            top_s = jnp.max(ms, axis=0, keepdims=True)
            fade = jnp.exp2((mt - top_t) * scale2)
            tot_t = jnp.sum(tot_t * fade, axis=0, keepdims=True)
            tot_s = jnp.sum(tot_s * jnp.exp2((ms - top_s) * scale2), axis=0, keepdims=True)
            mixed = jnp.sum(cross * fade, axis=0, keepdims=True)
            value = (mixed / tot_t + (top_s - top_t)) * scale + (jnp.log(tot_s) - jnp.log(tot_t))
            div = div + value[:, 0:128] + value[:, 128:256]
            log_t = jnp.log2(coef / tot_t)
            log_s = jnp.log2(coef / tot_s)

            def gradient(n, near):
                k0 = pl.multiple_of(n * CHUNK, CHUNK)
                pieces = []
                for g in range(0, CHUNK, 64):
                    at = pl.ds(pl.multiple_of(k0 + g, 64), 64)
                    pieces.append(
                        (
                            jnp.exp2((ss[at] - top_s) * scale2 + log_s)
                            - jnp.exp2((st[at] - top_t) * scale2 + log_t)
                        ).astype(BF16)
                    )
                g = jnp.concatenate(pieces, axis=0)
                columns = jnp.concatenate([kst[n * span + u] for u in range(span)], axis=1)
                acc[:, pl.ds(k0, CHUNK)] += lax.dot_general(bt, g, last_dims, preferred_element_type=F32)
                return near + jnp.dot(columns, g, preferred_element_type=F32)

            near = lax.fori_loop(lower, upper, gradient, jnp.zeros((64, ROWS), F32))
            acc[:, pl.ds(pl.multiple_of(r0, ROWS), ROWS)] += near
            return div

        div = lax.fori_loop(0, 4, one_block, jnp.zeros((1, 128), F32))
        tile = in_three(div)
        for row in range(NY):
            for parity in range(2):
                for i in range(4):
                    base = (row * NZ + 2 * i + parity) * TOK
                    part[row, parity, i * 64 : (i + 1) * 64] = (
                        acc[:, base : base + TOK] * jnp.float32(1.0 / 8.0)
                    ).astype(BF16)
                part[row, parity, 256:PART] = tile


def relate(lengths, keys):
    vmem = pl.BlockSpec(memory_space=pltpu.VMEM)
    smem = pl.BlockSpec(memory_space=pltpu.SMEM)
    return pl.pallas_call(
        relate_kernel,
        name="relate",
        out_shape=jax.ShapeDtypeStruct((NY, 2, PART, 128), BF16),
        in_specs=[smem, pl.BlockSpec(memory_space=pl.ANY)],
        out_specs=vmem,
        scratch_shapes=[
            pltpu.VMEM((SLOTS, TOK, 256), BF16),
            pltpu.VMEM((SLOTS, 64, TOK), BF16),
            pltpu.VMEM((SLOTS, TOK, 64), BF16),
            pltpu.VMEM((KEYS, ROWS), F32),
            pltpu.VMEM((KEYS, ROWS), F32),
            pltpu.VMEM((64, KEYS), F32),
            pltpu.SemaphoreType.DMA((3,)),
        ],
        compiler_params=pltpu.CompilerParams(vmem_limit_bytes=VMEM_LIMIT),
    )(lengths, keys)


def fold_kernel(
    part, cols, mean, both,
    in1, sums, in2, outp, in4, win, prev, follow, div_x, div_1, fetched,
    load, s1, r1, s2, r2, s4, r4, sw, rw, sv, rv, sx, rx,
):
    seq, head, y, z, x, c = place()
    ahead = (seq, (head + 1) % 8)
    behind = (seq, (head + 7) % 8)
    other = head + 1 - 2 * c
    fetch = pltpu.make_async_copy(cols, fetched, load)
    fetch.start()
    peers = [(seq, (head + d) % 8) for d in range(1, 8)]
    for dz in range(1, NZ):
        for h in (head, other):
            peers.append((y * NZ + (z + dz) % NZ, h))
    for dy in range(1, NY):
        for h in (head, other):
            peers.append((((y + dy) % NY) * NZ + z, h))
        peers.append((((y + dy) % NY) * NZ + z + 1 - 2 * (z % 2), head))
    greet(peers)()
    active = pair_at(z, y // 2) < PAIRS

    def row_copies():
        me = y * 2 + c
        copies = []
        for dy in (2, 1, 3):
            row = (y + dy) % NY
            for core in range(2):
                copies.append(
                    remote(part.at[row, core], in1.at[me], s1.at[2 * dy + core], r1.at[me], (row * NZ + z, 2 * x + core))
                )
        copies.append(remote(part.at[y, 1 - c], in1.at[me], s1.at[0], r1.at[me], (seq, other)))
        return copies

    @pl.when(active)
    def _():
        for copy in row_copies():
            copy.start()
        pltpu.make_async_copy(part.at[y, c], in1.at[y * 2 + c], r1.at[y * 2 + c]).start()

    def each_pair_copy(p, go):
        k = pair_at(z, p)
        for i in range(4):
            copy = remote(sums.at[p], in2.at[k], s2.at[p * 4 + i], r2.at[k], (y * NZ + 2 * i + c, 2 * x + p))
            mine = jnp.logical_and(c == p, z == 2 * i + c)

            @pl.when(jnp.logical_not(mine))
            def _():
                copy.start() if go else copy.wait_send()

            if go:
                @pl.when(mine)
                def _():
                    pltpu.make_async_copy(sums.at[p], in2.at[k], r2.at[k]).start()

    for p in range(2):
        @pl.when(pair_at(z, p) < PAIRS)
        def _():
            total = jnp.zeros((256, 128), F32)
            tiles = jnp.zeros((16, 128), F32)
            for n in range(4 * p, 4 * p + 4):
                pltpu.make_async_copy(in1.at[n], in1.at[n], r1.at[n]).wait()
                total = total + in1[n, 0:256].astype(F32)
                tiles = tiles + in1[n, 256:PART].astype(F32)
            sums[p, 0:256] = total.astype(BF16)
            sums[p, 256:PART] = in_three(jnp.sum(tiles, axis=0, keepdims=True))
            each_pair_copy(p, True)

    fetch.wait()
    tiles = jnp.zeros((16, 128), F32)
    for k in range(PAIRS):
        pltpu.make_async_copy(in2.at[k], in2.at[k], r2.at[k]).wait()
    for k in range(PAIRS):
        tiles = tiles + in2[k, 256:PART].astype(F32)
    grad = jnp.zeros((512, 384), F32)
    for i in range(4):
        grad = grad + lax.dot_general(
            fetched[:, i].reshape(512, TOK), in2[0:PAIRS, i * 64 : (i + 1) * 64].reshape(384, TOK),
            (((1,), (1,)), ((), ())),
            preferred_element_type=F32,
        )
    for n in range(8):
        outp[n] = grad[n * 64 : (n + 1) * 64].astype(BF16)

    slot = y * 2 + z % 2
    block_copies = []
    for d in (4, 5, 2, 3, 6, 7, 1):
        to = (slot + d) % 8
        block_copies.append(
            remote(
                outp.at[to], in4.at[slot], s4.at[d], r4.at[slot],
                ((to // 2) * NZ + (z // 2) * 2 + to % 2, head),
            )
        )
    for copy in block_copies:
        copy.start()
    pltpu.make_async_copy(outp.at[slot], in4.at[slot], r4.at[slot]).start()

    div_1[...] = jnp.broadcast_to(jnp.sum(tiles, axis=0, keepdims=True), (8, 128))
    pltpu.make_async_copy(div_1, div_x.at[head], rx.at[head]).start()
    div_copies = [remote(div_1, div_x.at[head], sx.at[d], rx.at[head], (seq, (head + d) % 8)) for d in range(1, 8)]
    for copy in div_copies:
        copy.start()

    total = jnp.zeros((64, 384), F32)
    for n in range(8):
        pltpu.make_async_copy(in4.at[n], in4.at[n], r4.at[n]).wait()
        total = total + in4[n].astype(F32)
    win[...] = total.astype(BF16)
    lasts = [remote(win, prev, sw, rw, ahead), remote(win, follow, sv, rv, behind)]
    for copy in lasts:
        copy.start()
    both[:, 384:768] = win[...]
    for copy in block_copies + div_copies:
        copy.wait_send()

    @pl.when(active)
    def _():
        for copy in row_copies():
            copy.wait_send()

    for p in range(2):
        @pl.when(pair_at(z, p) < PAIRS)
        def _():
            each_pair_copy(p, False)

    total = jnp.zeros((8, 128), F32)
    for n in range(8):
        pltpu.make_async_copy(div_x.at[n], div_x.at[n], rx.at[n]).wait()
        total = total + div_x[n]
    mean[0, 0] = jnp.sum(total[0:1]) * jnp.float32(1.0 / 196608.0)
    for copy in lasts:
        copy.wait_send()
        copy.wait_recv()
    both[:, 0:384] = prev[...]
    both[:, 768:1152] = follow[...]


def fold(part, cols):
    vmem = pl.BlockSpec(memory_space=pltpu.VMEM)
    smem = pl.BlockSpec(memory_space=pltpu.SMEM)
    dma = pltpu.SemaphoreType.DMA
    return pl.pallas_call(
        fold_kernel,
        name="fold",
        out_shape=(jax.ShapeDtypeStruct((1, 1), F32), jax.ShapeDtypeStruct((64, 1152), BF16)),
        in_specs=[pl.BlockSpec(memory_space=pl.ANY)] * 2,
        out_specs=(smem, vmem),
        scratch_shapes=[
            pltpu.VMEM((8, PART, 128), BF16),
            pltpu.VMEM((2, PART, 128), BF16),
            pltpu.VMEM((NZ, PART, 128), BF16),
            pltpu.VMEM((8, 64, 384), BF16),
            pltpu.VMEM((8, 64, 384), BF16),
            pltpu.VMEM((64, 384), BF16),
            pltpu.VMEM((64, 384), BF16),
            pltpu.VMEM((64, 384), BF16),
            pltpu.VMEM((8, 8, 128), F32),
            pltpu.VMEM((8, 128), F32),
            pltpu.VMEM((8, 4, 64, TOK), BF16),
            dma(()), dma((8,)), dma((8,)), dma((8,)), dma((NZ,)), dma((8,)), dma((8,)),
            dma(()), dma(()), dma(()), dma(()), dma((8,)), dma((8,)),
        ],
        compiler_params=pltpu.CompilerParams(
            collective_id=1, has_side_effects=True, vmem_limit_bytes=VMEM_LIMIT
        ),
    )(part, cols)


def shift_kernel(s_shift, both, gq, gk, gv):
    there = lax.broadcasted_iota(jnp.int32, (384, 128), 0)
    here = lax.broadcasted_iota(jnp.int32, (384, 128), 1)
    pick = jnp.where(there == here + (192 - s_shift[0]), jnp.float32(1.0), jnp.float32(0.0)).astype(BF16)
    for kind, out in enumerate((gq, gk, gv)):
        out[...] = functools.reduce(
            jnp.add,
            [
                jnp.dot(
                    both[:, 384 * n + 128 * kind : 384 * n + 128 * kind + 128],
                    pick[128 * n : 128 * n + 128],
                    preferred_element_type=F32,
                )
                for n in range(3)
            ],
        ).astype(BF16)


def shift(s_shift, both):
    vmem = pl.BlockSpec(memory_space=pltpu.VMEM)
    grad = jax.ShapeDtypeStruct((64, 128), BF16)
    return pl.pallas_call(
        shift_kernel,
        name="shift",
        out_shape=(grad, grad, grad),
        in_specs=[pl.BlockSpec(memory_space=pltpu.SMEM), vmem],
        out_specs=(vmem, vmem, vmem),
    )(s_shift, both)


def local(
    teacher_query, teacher_key, teacher_value, student_hidden, weight_query, weight_key, weight_value,
    teacher_shift, student_shift, segment_lengths,
):
    keys, cols = spread(
        teacher_shift, student_shift, teacher_query, teacher_key, teacher_value, student_hidden,
        weight_query, weight_key, weight_value,
    )
    mean, both = fold(relate(segment_lengths, keys), cols)
    return (mean[0, 0], *shift(student_shift, both))


def solution(mesh):
    in_specs = (
        P("seq", "head"),
        P("seq", "head"),
        P("seq", "head"),
        P("seq", None),
        P(None, "head"),
        P(None, "head"),
        P(None, "head"),
        P(),
        P(),
        P(),
    )
    out_specs = (P(), P("seq", "head"), P("seq", "head"), P("seq", "head"))
    return jax.shard_map(local, mesh=mesh, in_specs=in_specs, out_specs=out_specs, check_vma=False)
```

```python
import functools
import math

import jax
import jax.numpy as jnp
from jax import lax
from jax.experimental import pallas as pl
from jax.experimental.pallas import tpu as pltpu
from jax.sharding import PartitionSpec as P

MESH = pl.DeviceIdType.MESH
NEG = -1e30
TOK = 128
NZ = 8
NY = 4
PAIRS = 6
VMEM_LIMIT = 60 * 1024 * 1024
SLOTS = NY * NZ
PIECE = 320
ROWS = 256
CHUNK = 512
FLIGHT = 2
PART = 272
KEYS = SLOTS * TOK
F32 = jnp.float32
BF16 = jnp.bfloat16


def place():
    seq = lax.axis_index("seq")
    head = lax.axis_index("head")
    return seq, head, seq // NZ, seq % NZ, head // 2, head % 2


def pair_at(z, group):
    return (z + 4 * group) % NZ


def greet(peers):
    barrier = pltpu.get_barrier_semaphore()
    for peer in peers:
        pl.semaphore_signal(barrier, inc=1, device_id=peer, device_id_type=MESH)
    return lambda: pl.semaphore_wait(barrier, len(peers))


def remote(src, dst, send, recv, device):
    return pltpu.make_async_remote_copy(
        src_ref=src, dst_ref=dst, send_sem=send, recv_sem=recv, device_id=device, device_id_type=MESH
    )


def spread_kernel(
    t_shift, s_shift, tq, tk, tv, hidden, wq, wk, wv,
    keys, cols,
    stack, tokens, weights, small_n, small_p, stud, piece, transit, hid,
    load, n_send, n_recv, p_send, p_recv,
    k_send, key_sem, tr_sem, f_send, g_send, r_send, z_send, z_recv, h_send, h_recv,
):
    seq, head, y, z, x, c = place()
    sibling = (seq, head + 1 - 2 * c)
    behind = (seq, (head + 7) % 8)
    teachers = (tq, tk, tv)
    loads = [pltpu.make_async_copy(hidden, tokens, load.at[0])]
    for kind, weight in enumerate((wq, wk, wv)):
        loads.append(pltpu.make_async_copy(weight, weights.at[kind], load.at[1 + kind]))
    for kind in range(3):
        for j in range(2):
            loads.append(
                pltpu.make_async_copy(
                    teachers[kind].at[:, 128 * j : 128 * j + 384],
                    stack.at[2 * kind + j, :, 128 - 128 * j : 512 - 128 * j],
                    load.at[4 + 2 * kind + j],
                )
            )
    for copy in loads:
        copy.start()

    peers = [(seq, (head + d) % 8) for d in range(1, 8)]
    for dz in range(1, NZ):
        other = y * NZ + (z + dz) % NZ
        peers.append((other, head))
        peers.append((other, sibling[1]))
    for dy in range(1, NY):
        peers.append((((y + dy) % NY) * NZ + z, head))
    wait_all = greet(peers)

    loads[0].wait()
    for kind in range(3):
        loads[1 + kind].wait()
        stud[:, kind * 128 : (kind + 1) * 128] = jnp.dot(
            tokens[...], weights[kind], preferred_element_type=F32
        ).astype(BF16)
    wait_all()

    ahead = (seq, (head + 1) % 8)
    outs = []
    for kind in range(3):
        first, last = teachers[kind].at[:, 0:128], teachers[kind].at[:, 384:512]
        outs.append(
            remote(first, stack.at[2 * kind + 1, :, 384:512], n_send.at[kind], n_recv.at[kind], behind)
        )
        outs.append(remote(last, stack.at[2 * kind, :, 0:128], p_send.at[kind], p_recv.at[kind], ahead))
    outs.append(remote(stud, small_n, n_send.at[3], n_recv.at[3], behind))
    outs.append(remote(stud, small_p, p_send.at[3], p_recv.at[3], ahead))
    for copy in outs[6:] + outs[:6]:
        copy.start()

    for part in range(4):
        first = pl.multiple_of(head // 2 * 512 + part * 128, 128)
        hid[part] = jnp.transpose(tokens[:, pl.ds(first, 128)].astype(F32)).astype(BF16)
    mine = pl.ds(pl.multiple_of(c * 64, 64), 64)
    column_outs = []
    for d in range(1, 4):
        to = (z + 2 * d) % NZ
        column_outs.append(
            remote(
                hid.at[to // 2, mine], cols.at[head, z // 2], z_send.at[d], z_recv.at[z // 2], (y * NZ + to, head)
            )
        )
    for copy in column_outs:
        copy.start()
    pltpu.make_async_copy(hid.at[z // 2, mine], cols.at[head, z // 2], z_recv.at[z // 2]).start()

    def one_hot(rows, columns, first, dim):
        there = lax.broadcasted_iota(jnp.int32, (rows, columns), dim)
        here = lax.broadcasted_iota(jnp.int32, (rows, columns), 1 - dim)
        return jnp.where(there == here + first, jnp.float32(1.0), jnp.float32(0.0)).astype(BF16)

    pick_t = one_hot(512, 256, t_shift[0] - 128, 0)
    pick_s = (one_hot(64, 256, s_shift[0] + 64, 1), one_hot(64, 256, s_shift[0], 1))
    own_pair = c == y // 2
    core = z % 2

    def send_piece(to, go):
        k = pair_at(to, c)
        target = (y * NZ + to, 2 * x + core)
        some = k < PAIRS
        here = jnp.logical_and(some, jnp.logical_and(z == to, core == c))
        there = jnp.logical_and(some, jnp.logical_not(here))

        @pl.when(jnp.logical_and(own_pair, there))
        def _():
            copy = remote(piece.at[k], keys.at[seq], k_send.at[k], key_sem.at[seq], target)
            copy.start() if go else copy.wait_send()

        @pl.when(jnp.logical_and(jnp.logical_not(own_pair), there))
        def _():
            copy = remote(piece.at[k], transit.at[z // 2], k_send.at[k], tr_sem.at[z // 2], target)
            copy.start() if go else copy.wait_send()

        if go:
            @pl.when(jnp.logical_and(own_pair, here))
            def _():
                pltpu.make_async_copy(piece.at[k], keys.at[seq], key_sem.at[seq]).start()

            @pl.when(jnp.logical_and(jnp.logical_not(own_pair), here))
            def _():
                pltpu.make_async_copy(piece.at[k], transit.at[z // 2], tr_sem.at[z // 2]).start()

    transposed = (((1,), (1,)), ((), ()))
    for copy in outs[6:]:
        copy.wait_recv()
    for k in range(PAIRS):
        at = slice(k // 2 * 128, (k // 2 + 1) * 128)
        before, after = (small_p, stud) if k % 2 == 0 else (stud, small_n)
        pick = pick_s[k % 2]
        small = lax.dot_general(
            pick[:, 0:128], before[:, at], transposed, preferred_element_type=F32
        ) + lax.dot_general(pick[:, 128:256], after[:, at], transposed, preferred_element_type=F32)
        piece[k, 256:320] = small.astype(BF16)
    for copy in loads[4:]:
        copy.wait()
    for copy in outs[:6]:
        copy.wait_recv()
    window = jnp.dot(stack[...].reshape(PAIRS * TOK, 512), pick_t, preferred_element_type=F32)
    for k in range(PAIRS):
        piece[k, 0:128] = window[k * TOK : (k + 1) * TOK, 0:128].astype(BF16)
        piece[k, 128:256] = window[k * TOK : (k + 1) * TOK, 128:256].astype(BF16)
    order = [(z + d + NZ) % NZ for d in (0, 1, -1, 2, -2, 3, -3, 4)]
    for n, to in enumerate(order):
        if n > FLIGHT:
            send_piece(order[n - 1 - FLIGHT], False)
        send_piece(to, True)

    active = pair_at(z, y // 2) < PAIRS
    passing = pair_at(z, 1 - y // 2) < PAIRS
    beside = y + 1 - 2 * (y % 2)
    partner = (beside * NZ + z, head)
    opposite = ((3 - y) * NZ + z, head)

    def key_copy(slot, send, device):
        return remote(keys.at[slot], keys.at[slot], send, key_sem.at[slot], device)

    def source(turn):
        same = (0, 2, 6, 4)[turn]
        cross = (1, 7, 3, 5)[turn]
        return (z + jnp.where(core == c, same, cross)) % NZ

    def forwards(turn):
        slot = y * NZ + source(turn)
        return key_copy(slot, f_send.at[turn], partner), key_copy(slot, r_send.at[turn], sibling)

    def passed(turn):
        slot = y * NZ + source(turn)
        i = source(turn) // 2
        return i, [
            remote(
                transit.at[i], keys.at[slot], g_send.at[2 * turn + n], key_sem.at[slot],
                ((row * NZ) + z, head),
            )
            for n, row in enumerate((3 - y, 3 - beside))
        ]

    for turn in range(4):
        @pl.when(passing)
        def _():
            i, copies = passed(turn)
            remote(transit.at[i], transit.at[i], g_send.at[2 * turn], tr_sem.at[i], partner).wait_recv()
            for copy in copies:
                copy.start()

        @pl.when(active)
        def _():
            first, relay = forwards(turn)
            first.wait_recv()
            first.start()
            relay.start()

    for i in range(4):
        pltpu.make_async_copy(hid.at[i, mine], cols.at[head, i], z_recv.at[i]).wait()
    head_outs = []
    for d in range(1, 8):
        head_outs.append(
            remote(cols.at[head], cols.at[head], h_send.at[d], h_recv.at[head], (seq, (head + d) % 8))
        )
    for copy in head_outs:
        copy.start()

    @pl.when(active)
    def _():
        for turn in range(4):
            for n, row in enumerate((beside, 3 - y, 3 - beside)):
                relay = key_copy(row * NZ + source(turn), r_send.at[4 + 3 * turn + n], sibling)
                relay.wait_recv()
                relay.start()
        for i in range(4):
            for row in range(NY):
                key_copy(row * NZ + 2 * i + 1 - c, r_send.at[0], sibling).wait_recv()
        for turn in range(4):
            key_copy(0, f_send.at[turn], partner).wait_send()
        for n in range(16):
            key_copy(0, r_send.at[n], sibling).wait_send()

    @pl.when(passing)
    def _():
        for turn in range(4):
            for copy in passed(turn)[1]:
                copy.wait_send()

    for d in range(1, 8):
        other = (head + d) % 8
        remote(cols.at[other], cols.at[other], h_send.at[d], h_recv.at[other], sibling).wait_recv()
    for copy in head_outs + column_outs + outs:
        copy.wait_send()
    for to in order[NZ - 1 - FLIGHT :]:
        send_piece(to, False)


def spread(t_shift, s_shift, tq, tk, tv, hidden, wq, wk, wv):
    anywhere = pl.BlockSpec(memory_space=pl.ANY)
    smem = pl.BlockSpec(memory_space=pltpu.SMEM)
    dma = pltpu.SemaphoreType.DMA
    return pl.pallas_call(
        spread_kernel,
        name="spread",
        out_shape=(
            jax.ShapeDtypeStruct((SLOTS, PIECE, 128), BF16),
            jax.ShapeDtypeStruct((8, 4, 64, TOK), BF16),
        ),
        in_specs=[smem, smem] + [anywhere] * 7,
        out_specs=(anywhere, anywhere),
        scratch_shapes=[
            pltpu.VMEM((PAIRS, TOK, 512), BF16),
            pltpu.VMEM((TOK, 2048), BF16),
            pltpu.VMEM((3, 2048, 128), BF16),
            pltpu.VMEM((TOK, 384), BF16),
            pltpu.VMEM((TOK, 384), BF16),
            pltpu.VMEM((TOK, 384), BF16),
            pltpu.VMEM((NZ, PIECE, 128), BF16),
            pltpu.VMEM((4, PIECE, 128), BF16),
            pltpu.VMEM((4, 128, TOK), BF16),
            dma((10,)), dma((4,)), dma((4,)), dma((4,)), dma((4,)),
            dma((NZ,)), dma((SLOTS,)), dma((4,)), dma((4,)), dma((8,)), dma((16,)),
            dma((4,)), dma((4,)), dma((8,)), dma((8,)),
        ],
        compiler_params=pltpu.CompilerParams(
            collective_id=0, has_side_effects=True, vmem_limit_bytes=VMEM_LIMIT
        ),
    )(t_shift, s_shift, tq, tk, tv, hidden, wq, wk, wv)


def in_three(row):
    high = row.astype(BF16).astype(F32)
    middle = (row - high).astype(BF16).astype(F32)
    low = row - high - middle
    at = lax.broadcasted_iota(jnp.int32, (16, 128), 0)
    tile = jnp.where(at == 0, high, jnp.where(at == 1, middle, jnp.where(at == 2, low, jnp.float32(0.0))))
    return tile.astype(BF16)


def relate_kernel(lengths, keys, part, kt, kst, ks, st, ss, acc, load):
    _, _, y, z, _, c = place()
    group = 2 * (y % 2) + c
    coef = jnp.float32(1.0 / 48.0)
    scale = jnp.float32(1.0 / 16.0)
    scale2 = jnp.float32(math.log2(math.e) / 16.0)
    two = ROWS // TOK
    blocks = KEYS // ROWS
    last_dims = (((1,), (1,)), ((), ()))

    @pl.when(pair_at(z, y // 2) < PAIRS)
    def _():
        loads = [
            pltpu.make_async_copy(keys.at[:, 256:320], kst, load.at[2]),
            pltpu.make_async_copy(keys.at[:, 0:128], kt.at[:, :, 0:128], load.at[0]),
            pltpu.make_async_copy(keys.at[:, 128:256], kt.at[:, :, 128:256], load.at[1]),
        ]
        for copy in loads:
            copy.start()
        acc[...] = jnp.zeros_like(acc)
        end0 = lengths[0]
        end1 = end0 + lengths[1]
        end2 = end1 + lengths[2]

        def first_of(position):
            zero = jnp.int32(0)
            start = jnp.where(position >= end0, end0, zero)
            start = jnp.where(position >= end1, end1, start)
            return jnp.where(position >= end2, end2, start)

        most = jnp.maximum(jnp.maximum(lengths[0], lengths[1]), jnp.maximum(lengths[2], lengths[3]))
        last = jnp.where(
            lengths[0] == most, end0, jnp.where(lengths[1] == most, end1, jnp.where(lengths[2] == most, end2, KEYS))
        )
        last_block = (last - 1) // ROWS
        unit = jnp.where(
            lax.broadcasted_iota(jnp.int32, (TOK, TOK), 0) == lax.broadcasted_iota(jnp.int32, (TOK, TOK), 1),
            jnp.float32(1.0),
            jnp.float32(0.0),
        ).astype(BF16)
        loads[0].wait()

        @pl.loop(0, SLOTS // 8)
        def _(n):
            for u in range(8):
                ks[8 * n + u] = lax.dot_general(
                    unit, kst[8 * n + u], last_dims, preferred_element_type=F32
                ).astype(BF16)

        for copy in loads[1:]:
            copy.wait()

        def one_block(t, div):
            odd = t % 2
            nth = 4 * t + odd * 3 + (1 - 2 * odd) * group
            block = (last_block + blocks - nth) % blocks
            r0 = block * ROWS
            lower = first_of(r0) // ROWS
            upper = block + 1
            latest = first_of(r0 + ROWS - 1)
            row = r0 + lax.broadcasted_iota(jnp.int32, (8, ROWS), 1)
            start = first_of(row)
            sub_row = lax.broadcasted_iota(jnp.int32, (8, ROWS), 0)
            bt = jnp.concatenate([kst[block * two + u] for u in range(two)], axis=1)
            b2 = (bt.astype(F32) * jnp.float32(2.0)).astype(BF16)

            def online(n, carry, width, mask):
                mt, ms, tot_t, tot_s, cross = carry
                k0 = pl.multiple_of(n * ROWS, ROWS)
                slots = pl.ds(n * two, width // TOK)
                a = lax.dot_general(
                    kt[slots].reshape(width, 256),
                    kt[pl.ds(block * two, two)].reshape(ROWS, 256),
                    last_dims,
                    preferred_element_type=F32,
                )
                b = jnp.dot(ks[slots].reshape(width, 64), b2, preferred_element_type=F32)
                for first in range(0, width, 64):
                    xs, ws = [], []
                    new_t, new_s = mt, ms
                    for g in range(first, first + 64, 8):
                        x = a[g : g + 8]
                        w = b[g : g + 8]
                        if mask:
                            column = sub_row + (k0 + g)
                            allowed = jnp.logical_and(column >= start, column <= row)
                            x = jnp.where(allowed, x, NEG)
                            w = jnp.where(allowed, w, NEG)
                        st[pl.ds(pl.multiple_of(k0 + g, 8), 8)] = x
                        ss[pl.ds(pl.multiple_of(k0 + g, 8), 8)] = w
                        new_t = jnp.maximum(new_t, x)
                        new_s = jnp.maximum(new_s, w)
                        xs.append(x)
                        ws.append(w)
                    fade = jnp.exp2((mt - new_t) * scale2)
                    tot_t = tot_t * fade
                    cross = cross * fade
                    tot_s = tot_s * jnp.exp2((ms - new_s) * scale2)
                    mt, ms = new_t, new_s
                    for x, w in zip(xs, ws):
                        ea = jnp.exp2((x - mt) * scale2)
                        tot_t = tot_t + ea
                        tot_s = tot_s + jnp.exp2((w - ms) * scale2)
                        cross = cross + ea * (x - w)
                return mt, ms, tot_t, tot_s, cross

            inner = jnp.minimum((latest + ROWS - 1) // ROWS, upper)
            wide = (jnp.maximum(block, inner) - inner) // 2
            narrow = upper - lower - 2 * wide

            def nth_narrow(n):
                return jnp.where(lower + n < inner, lower + n, lower + n + 2 * wide)

            low = jnp.full((8, ROWS), NEG, F32)
            zero = jnp.zeros((8, ROWS), F32)
            carry = lax.fori_loop(
                0, narrow, lambda n, carry: online(nth_narrow(n), carry, ROWS, True), (low, low, zero, zero, zero)
            )
            mt, ms, tot_t, tot_s, cross = lax.fori_loop(
                0, wide, lambda n, carry: online(inner + 2 * n, carry, CHUNK, False), carry
            )
            top_t = jnp.max(mt, axis=0, keepdims=True)
            top_s = jnp.max(ms, axis=0, keepdims=True)
            fade = jnp.exp2((mt - top_t) * scale2)
            tot_t = jnp.sum(tot_t * fade, axis=0, keepdims=True)
            tot_s = jnp.sum(tot_s * jnp.exp2((ms - top_s) * scale2), axis=0, keepdims=True)
            mixed = jnp.sum(cross * fade, axis=0, keepdims=True)
            value = (mixed / tot_t + (top_s - top_t)) * scale + (jnp.log(tot_s) - jnp.log(tot_t))
            div = div + value[:, 0:128] + value[:, 128:256]
            log_t = jnp.log2(coef / tot_t)
            log_s = jnp.log2(coef / tot_s)

            def gradient(n, near, width):
                k0 = pl.multiple_of(n * ROWS, ROWS)
                pieces = []
                for g in range(0, width, 64):
                    at = pl.ds(pl.multiple_of(k0 + g, 64), 64)
                    pieces.append(
                        (
                            jnp.exp2((ss[at] - top_s) * scale2 + log_s)
                            - jnp.exp2((st[at] - top_t) * scale2 + log_t)
                        ).astype(BF16)
                    )
                g = jnp.concatenate(pieces, axis=0)
                columns = jnp.concatenate([kst[n * two + u] for u in range(width // TOK)], axis=1)
                acc[:, pl.ds(k0, width)] += lax.dot_general(bt, g, last_dims, preferred_element_type=F32)
                return near + jnp.dot(columns, g, preferred_element_type=F32)

            near = lax.fori_loop(
                0, narrow, lambda n, near: gradient(nth_narrow(n), near, ROWS), jnp.zeros((64, ROWS), F32)
            )
            near = lax.fori_loop(0, wide, lambda n, near: gradient(inner + 2 * n, near, CHUNK), near)
            acc[:, pl.ds(pl.multiple_of(r0, ROWS), ROWS)] += near
            return div

        div = lax.fori_loop(0, 4, one_block, jnp.zeros((1, 128), F32))
        tile = in_three(div)
        for row in range(NY):
            for parity in range(2):
                for i in range(4):
                    base = (row * NZ + 2 * i + parity) * TOK
                    part[parity, row, i * 64 : (i + 1) * 64] = (
                        acc[:, base : base + TOK] * jnp.float32(1.0 / 8.0)
                    ).astype(BF16)
                part[parity, row, 256:PART] = tile


def relate(lengths, keys):
    vmem = pl.BlockSpec(memory_space=pltpu.VMEM)
    smem = pl.BlockSpec(memory_space=pltpu.SMEM)
    return pl.pallas_call(
        relate_kernel,
        name="relate",
        out_shape=jax.ShapeDtypeStruct((2, NY, PART, 128), BF16),
        in_specs=[smem, pl.BlockSpec(memory_space=pl.ANY)],
        out_specs=vmem,
        scratch_shapes=[
            pltpu.VMEM((SLOTS, TOK, 256), BF16),
            pltpu.VMEM((SLOTS, 64, TOK), BF16),
            pltpu.VMEM((SLOTS, TOK, 64), BF16),
            pltpu.VMEM((KEYS, ROWS), F32),
            pltpu.VMEM((KEYS, ROWS), F32),
            pltpu.VMEM((64, KEYS), F32),
            pltpu.SemaphoreType.DMA((3,)),
        ],
        compiler_params=pltpu.CompilerParams(vmem_limit_bytes=VMEM_LIMIT),
    )(lengths, keys)


def fold_kernel(
    part, cols, mean, both,
    own, in0, pre, in1, sums, in2, outp, in4, win, prev, follow, div_x, div_1, fetched,
    load, l0, s0, r0, s1, r1, s2, r2, s4, r4, sw, rw, sv, rv, sx, rx,
):
    seq, head, y, z, x, c = place()
    ahead = (seq, (head + 1) % 8)
    behind = (seq, (head + 7) % 8)
    other = head + 1 - 2 * c
    fetch = pltpu.make_async_copy(cols, fetched, load)
    fetch.start()
    active = pair_at(z, y // 2) < PAIRS
    mine = pltpu.make_async_copy(part.at[c], own, l0)

    @pl.when(active)
    def _():
        mine.start()

    peers = [(seq, (head + d) % 8) for d in range(1, 8)]
    for dz in range(1, NZ):
        for h in (head, other):
            peers.append((y * NZ + (z + dz) % NZ, h))
    for dy in range(1, NY):
        peers.append((((y + dy) % NY) * NZ + z, head))
        peers.append((((y + dy) % NY) * NZ + z + 1 - 2 * (z % 2), head))
    greet(peers)()
    across = remote(part.at[1 - c], in0, s0, r0, (seq, other))
    row_copies = [
        remote(pre.at[(y + dy) % NY], in1.at[y], s1.at[dy], r1.at[y], (((y + dy) % NY) * NZ + z, head))
        for dy in (2, 1, 3)
    ]

    @pl.when(active)
    def _():
        across.start()
        mine.wait()
        across.wait_recv()
        for turn in range(NY):
            row = (y + (2, 1, 3, 0)[turn]) % NY
            pre[row, 0:256] = (own[row, 0:256].astype(F32) + in0[row, 0:256].astype(F32)).astype(BF16)
            tiles = own[row, 256:PART].astype(F32) + in0[row, 256:PART].astype(F32)
            pre[row, 256:PART] = in_three(jnp.sum(tiles, axis=0, keepdims=True))
            if turn < 3:
                row_copies[turn].start()
            else:
                pltpu.make_async_copy(pre.at[y], in1.at[y], r1.at[y]).start()

    def each_pair_copy(p, go):
        k = pair_at(z, p)
        for i in range(4):
            copy = remote(sums.at[p], in2.at[k], s2.at[p * 4 + i], r2.at[k], (y * NZ + 2 * i + c, 2 * x + p))
            mine = jnp.logical_and(c == p, z == 2 * i + c)

            @pl.when(jnp.logical_not(mine))
            def _():
                copy.start() if go else copy.wait_send()

            if go:
                @pl.when(mine)
                def _():
                    pltpu.make_async_copy(sums.at[p], in2.at[k], r2.at[k]).start()

    for p in range(2):
        @pl.when(pair_at(z, p) < PAIRS)
        def _():
            total = jnp.zeros((256, 128), F32)
            tiles = jnp.zeros((16, 128), F32)
            for n in range(2 * p, 2 * p + 2):
                pltpu.make_async_copy(in1.at[n], in1.at[n], r1.at[n]).wait()
                total = total + in1[n, 0:256].astype(F32)
                tiles = tiles + in1[n, 256:PART].astype(F32)
            sums[p, 0:256] = total.astype(BF16)
            sums[p, 256:PART] = in_three(jnp.sum(tiles, axis=0, keepdims=True))
            each_pair_copy(p, True)

    fetch.wait()
    tiles = jnp.zeros((16, 128), F32)
    for k in range(PAIRS):
        pltpu.make_async_copy(in2.at[k], in2.at[k], r2.at[k]).wait()
    for k in range(PAIRS):
        tiles = tiles + in2[k, 256:PART].astype(F32)
    grad = jnp.zeros((512, 384), F32)
    for i in range(4):
        grad = grad + lax.dot_general(
            fetched[:, i].reshape(512, TOK), in2[0:PAIRS, i * 64 : (i + 1) * 64].reshape(384, TOK),
            (((1,), (1,)), ((), ())),
            preferred_element_type=F32,
        )
    for n in range(8):
        outp[n] = grad[n * 64 : (n + 1) * 64].astype(BF16)

    slot = y * 2 + z % 2
    block_copies = []
    for d in (4, 5, 2, 3, 6, 7, 1):
        to = (slot + d) % 8
        block_copies.append(
            remote(
                outp.at[to], in4.at[slot], s4.at[d], r4.at[slot],
                ((to // 2) * NZ + (z // 2) * 2 + to % 2, head),
            )
        )
    for copy in block_copies:
        copy.start()
    pltpu.make_async_copy(outp.at[slot], in4.at[slot], r4.at[slot]).start()

    div_1[...] = jnp.broadcast_to(jnp.sum(tiles, axis=0, keepdims=True), (8, 128))
    pltpu.make_async_copy(div_1, div_x.at[head], rx.at[head]).start()
    div_copies = [remote(div_1, div_x.at[head], sx.at[d], rx.at[head], (seq, (head + d) % 8)) for d in range(1, 8)]
    for copy in div_copies:
        copy.start()

    total = jnp.zeros((64, 384), F32)
    for n in range(8):
        pltpu.make_async_copy(in4.at[n], in4.at[n], r4.at[n]).wait()
        total = total + in4[n].astype(F32)
    win[...] = total.astype(BF16)
    lasts = [remote(win, prev, sw, rw, ahead), remote(win, follow, sv, rv, behind)]
    for copy in lasts:
        copy.start()
    both[:, 384:768] = win[...]
    for copy in block_copies + div_copies:
        copy.wait_send()

    @pl.when(active)
    def _():
        across.wait_send()
        for copy in row_copies:
            copy.wait_send()

    for p in range(2):
        @pl.when(pair_at(z, p) < PAIRS)
        def _():
            each_pair_copy(p, False)

    total = jnp.zeros((8, 128), F32)
    for n in range(8):
        pltpu.make_async_copy(div_x.at[n], div_x.at[n], rx.at[n]).wait()
        total = total + div_x[n]
    mean[0, 0] = jnp.sum(total[0:1]) * jnp.float32(1.0 / 196608.0)
    for copy in lasts:
        copy.wait_send()
        copy.wait_recv()
    both[:, 0:384] = prev[...]
    both[:, 768:1152] = follow[...]


def fold(part, cols):
    vmem = pl.BlockSpec(memory_space=pltpu.VMEM)
    smem = pl.BlockSpec(memory_space=pltpu.SMEM)
    dma = pltpu.SemaphoreType.DMA
    return pl.pallas_call(
        fold_kernel,
        name="fold",
        out_shape=(jax.ShapeDtypeStruct((1, 1), F32), jax.ShapeDtypeStruct((64, 1152), BF16)),
        in_specs=[pl.BlockSpec(memory_space=pl.ANY)] * 2,
        out_specs=(smem, vmem),
        scratch_shapes=[
            pltpu.VMEM((NY, PART, 128), BF16),
            pltpu.VMEM((NY, PART, 128), BF16),
            pltpu.VMEM((NY, PART, 128), BF16),
            pltpu.VMEM((NY, PART, 128), BF16),
            pltpu.VMEM((2, PART, 128), BF16),
            pltpu.VMEM((NZ, PART, 128), BF16),
            pltpu.VMEM((8, 64, 384), BF16),
            pltpu.VMEM((8, 64, 384), BF16),
            pltpu.VMEM((64, 384), BF16),
            pltpu.VMEM((64, 384), BF16),
            pltpu.VMEM((64, 384), BF16),
            pltpu.VMEM((8, 8, 128), F32),
            pltpu.VMEM((8, 128), F32),
            pltpu.VMEM((8, 4, 64, TOK), BF16),
            dma(()), dma(()), dma(()), dma(()), dma((NY,)), dma((NY,)), dma((8,)), dma((NZ,)), dma((8,)), dma((8,)),
            dma(()), dma(()), dma(()), dma(()), dma((8,)), dma((8,)),
        ],
        compiler_params=pltpu.CompilerParams(
            collective_id=1, has_side_effects=True, vmem_limit_bytes=VMEM_LIMIT
        ),
    )(part, cols)


def shift_kernel(s_shift, both, gq, gk, gv):
    there = lax.broadcasted_iota(jnp.int32, (384, 128), 0)
    here = lax.broadcasted_iota(jnp.int32, (384, 128), 1)
    pick = jnp.where(there == here + (192 - s_shift[0]), jnp.float32(1.0), jnp.float32(0.0)).astype(BF16)
    for kind, out in enumerate((gq, gk, gv)):
        out[...] = functools.reduce(
            jnp.add,
            [
                jnp.dot(
                    both[:, 384 * n + 128 * kind : 384 * n + 128 * kind + 128],
                    pick[128 * n : 128 * n + 128],
                    preferred_element_type=F32,
                )
                for n in range(3)
            ],
        ).astype(BF16)


def shift(s_shift, both):
    vmem = pl.BlockSpec(memory_space=pltpu.VMEM)
    grad = jax.ShapeDtypeStruct((64, 128), BF16)
    return pl.pallas_call(
        shift_kernel,
        name="shift",
        out_shape=(grad, grad, grad),
        in_specs=[pl.BlockSpec(memory_space=pltpu.SMEM), vmem],
        out_specs=(vmem, vmem, vmem),
    )(s_shift, both)


def local(
    teacher_query, teacher_key, teacher_value, student_hidden, weight_query, weight_key, weight_value,
    teacher_shift, student_shift, segment_lengths,
):
    keys, cols = spread(
        teacher_shift, student_shift, teacher_query, teacher_key, teacher_value, student_hidden,
        weight_query, weight_key, weight_value,
    )
    mean, both = fold(relate(segment_lengths, keys), cols)
    return (mean[0, 0], *shift(student_shift, both))


def solution(mesh):
    in_specs = (
        P("seq", "head"),
        P("seq", "head"),
        P("seq", "head"),
        P("seq", None),
        P(None, "head"),
        P(None, "head"),
        P(None, "head"),
        P(),
        P(),
        P(),
    )
    out_specs = (P(), P("seq", "head"), P("seq", "head"), P("seq", "head"))
    return jax.shard_map(local, mesh=mesh, in_specs=in_specs, out_specs=out_specs, check_vma=False)
```

```python
import functools
import math

import jax
import jax.numpy as jnp
from jax import lax
from jax.experimental import pallas as pl
from jax.experimental.pallas import tpu as pltpu
from jax.sharding import PartitionSpec as P

MESH = pl.DeviceIdType.MESH
NEG = -1e30
TOK = 128
NZ = 8
NY = 4
PAIRS = 6
VMEM_LIMIT = 60 * 1024 * 1024
SLOTS = NY * NZ
PIECE = 320
ROWS = 256
CHUNK = 512
FLIGHT = 2
PART = 272
KEYS = SLOTS * TOK
F32 = jnp.float32
BF16 = jnp.bfloat16


def place():
    seq = lax.axis_index("seq")
    head = lax.axis_index("head")
    return seq, head, seq // NZ, seq % NZ, head // 2, head % 2


def pair_at(z, group):
    return (z + 4 * group) % NZ


def greet(peers):
    barrier = pltpu.get_barrier_semaphore()
    for peer in peers:
        pl.semaphore_signal(barrier, inc=1, device_id=peer, device_id_type=MESH)
    return lambda: pl.semaphore_wait(barrier, len(peers))


def remote(src, dst, send, recv, device):
    return pltpu.make_async_remote_copy(
        src_ref=src, dst_ref=dst, send_sem=send, recv_sem=recv, device_id=device, device_id_type=MESH
    )


def spread_kernel(
    t_shift, s_shift, tq, tk, tv, hidden, wq, wk, wv,
    keys, cols,
    stack, tokens, weights, small_n, small_p, stud, piece, transit, hid,
    load, n_send, n_recv, p_send, p_recv,
    k_send, key_sem, tr_sem, f_send, g_send, r_send, z_send, z_recv, h_send, h_recv,
):
    seq, head, y, z, x, c = place()
    sibling = (seq, head + 1 - 2 * c)
    behind = (seq, (head + 7) % 8)
    teachers = (tq, tk, tv)
    loads = [pltpu.make_async_copy(hidden, tokens, load.at[0])]
    for kind, weight in enumerate((wq, wk, wv)):
        loads.append(pltpu.make_async_copy(weight, weights.at[:, kind * 128 : (kind + 1) * 128], load.at[1 + kind]))
    for kind in range(3):
        for j in range(2):
            loads.append(
                pltpu.make_async_copy(
                    teachers[kind].at[:, 128 * j : 128 * j + 384],
                    stack.at[2 * kind + j, :, 128 - 128 * j : 512 - 128 * j],
                    load.at[4 + 2 * kind + j],
                )
            )
    for copy in loads:
        copy.start()

    peers = [(seq, (head + d) % 8) for d in range(1, 8)]
    for dz in range(1, NZ):
        other = y * NZ + (z + dz) % NZ
        peers.append((other, head))
        peers.append((other, sibling[1]))
    for dy in range(1, NY):
        peers.append((((y + dy) % NY) * NZ + z, head))
    wait_all = greet(peers)

    wait_all()

    ahead = (seq, (head + 1) % 8)
    outs = []
    for kind in range(3):
        first, last = teachers[kind].at[:, 0:128], teachers[kind].at[:, 384:512]
        outs.append(
            remote(first, stack.at[2 * kind + 1, :, 384:512], n_send.at[kind], n_recv.at[kind], behind)
        )
        outs.append(remote(last, stack.at[2 * kind, :, 0:128], p_send.at[kind], p_recv.at[kind], ahead))
    outs.append(remote(stud, small_n.at[:, 128:256], n_send.at[3], n_recv.at[3], behind))
    outs.append(remote(stud, small_p.at[:, 0:128], p_send.at[3], p_recv.at[3], ahead))
    for copy in outs[:6]:
        copy.start()

    loads[0].wait()
    for copy in loads[1:4]:
        copy.wait()
    projected = jnp.dot(tokens[...], weights[...], preferred_element_type=F32)
    for kind in range(3):
        rows = slice(kind * TOK, (kind + 1) * TOK)
        values = projected[:, kind * 128 : (kind + 1) * 128].astype(BF16)
        stud[rows] = values
        small_p[rows, 128:256] = values
        small_n[rows, 0:128] = values
    for copy in outs[6:]:
        copy.start()

    for part in range(4):
        first = pl.multiple_of(head // 2 * 512 + part * 128, 128)
        hid[part] = jnp.transpose(tokens[:, pl.ds(first, 128)].astype(F32)).astype(BF16)
    mine = pl.ds(pl.multiple_of(c * 64, 64), 64)
    column_outs = []
    for d in range(1, 4):
        to = (z + 2 * d) % NZ
        column_outs.append(
            remote(
                hid.at[to // 2, mine], cols.at[head, z // 2], z_send.at[d], z_recv.at[z // 2], (y * NZ + to, head)
            )
        )
    for copy in column_outs:
        copy.start()
    pltpu.make_async_copy(hid.at[z // 2, mine], cols.at[head, z // 2], z_recv.at[z // 2]).start()

    def one_hot(rows, columns, first, dim):
        there = lax.broadcasted_iota(jnp.int32, (rows, columns), dim)
        here = lax.broadcasted_iota(jnp.int32, (rows, columns), 1 - dim)
        return jnp.where(there == here + first, jnp.float32(1.0), jnp.float32(0.0)).astype(BF16)

    pick_t = one_hot(512, 256, t_shift[0] - 128, 0)
    pick_s = (one_hot(64, 256, s_shift[0] + 64, 1), one_hot(64, 256, s_shift[0], 1))
    own_pair = c == y // 2
    core = z % 2

    def send_piece(to, go):
        k = pair_at(to, c)
        target = (y * NZ + to, 2 * x + core)
        some = k < PAIRS
        here = jnp.logical_and(some, jnp.logical_and(z == to, core == c))
        there = jnp.logical_and(some, jnp.logical_not(here))

        @pl.when(jnp.logical_and(own_pair, there))
        def _():
            copy = remote(piece.at[k], keys.at[seq], k_send.at[k], key_sem.at[seq], target)
            copy.start() if go else copy.wait_send()

        @pl.when(jnp.logical_and(jnp.logical_not(own_pair), there))
        def _():
            copy = remote(piece.at[k], transit.at[z // 2], k_send.at[k], tr_sem.at[z // 2], target)
            copy.start() if go else copy.wait_send()

        if go:
            @pl.when(jnp.logical_and(own_pair, here))
            def _():
                pltpu.make_async_copy(piece.at[k], keys.at[seq], key_sem.at[seq]).start()

            @pl.when(jnp.logical_and(jnp.logical_not(own_pair), here))
            def _():
                pltpu.make_async_copy(piece.at[k], transit.at[z // 2], tr_sem.at[z // 2]).start()

    transposed = (((1,), (1,)), ((), ()))
    for copy in loads[4:]:
        copy.wait()
    for copy in outs[:6]:
        copy.wait_recv()
    window = jnp.dot(stack[...].reshape(PAIRS * TOK, 512), pick_t, preferred_element_type=F32)
    for k in range(PAIRS):
        piece[k, 0:128] = window[k * TOK : (k + 1) * TOK, 0:128].astype(BF16)
        piece[k, 128:256] = window[k * TOK : (k + 1) * TOK, 128:256].astype(BF16)
    for copy in outs[6:]:
        copy.wait_recv()
    for j, joined in enumerate((small_p, small_n)):
        small = lax.dot_general(pick_s[j], joined[...], transposed, preferred_element_type=F32)
        for kind in range(3):
            piece[2 * kind + j, 256:320] = small[:, kind * TOK : (kind + 1) * TOK].astype(BF16)
    order = [(z + d + NZ) % NZ for d in (0, 1, -1, 2, -2, 3, -3, 4)]
    for n, to in enumerate(order):
        if n > FLIGHT:
            send_piece(order[n - 1 - FLIGHT], False)
        send_piece(to, True)

    active = pair_at(z, y // 2) < PAIRS
    passing = pair_at(z, 1 - y // 2) < PAIRS
    beside = y + 1 - 2 * (y % 2)
    partner = (beside * NZ + z, head)
    opposite = ((3 - y) * NZ + z, head)

    def key_copy(slot, send, device):
        return remote(keys.at[slot], keys.at[slot], send, key_sem.at[slot], device)

    def source(turn):
        same = (0, 2, 6, 4)[turn]
        cross = (1, 7, 3, 5)[turn]
        return (z + jnp.where(core == c, same, cross)) % NZ

    def forwards(turn):
        slot = y * NZ + source(turn)
        return key_copy(slot, f_send.at[turn], partner), key_copy(slot, r_send.at[turn], sibling)

    def passed(turn):
        slot = y * NZ + source(turn)
        i = source(turn) // 2
        return i, [
            remote(
                transit.at[i], keys.at[slot], g_send.at[2 * turn + n], key_sem.at[slot],
                ((row * NZ) + z, head),
            )
            for n, row in enumerate((3 - y, 3 - beside))
        ]

    for turn in range(4):
        @pl.when(passing)
        def _():
            i, copies = passed(turn)
            remote(transit.at[i], transit.at[i], g_send.at[2 * turn], tr_sem.at[i], partner).wait_recv()
            for copy in copies:
                copy.start()

        @pl.when(active)
        def _():
            first, relay = forwards(turn)
            first.wait_recv()
            first.start()
            relay.start()

    for i in range(4):
        pltpu.make_async_copy(hid.at[i, mine], cols.at[head, i], z_recv.at[i]).wait()
    head_outs = []
    for d in range(1, 8):
        head_outs.append(
            remote(cols.at[head], cols.at[head], h_send.at[d], h_recv.at[head], (seq, (head + d) % 8))
        )
    for copy in head_outs:
        copy.start()

    @pl.when(active)
    def _():
        for turn in range(4):
            for n, row in enumerate((beside, 3 - y, 3 - beside)):
                relay = key_copy(row * NZ + source(turn), r_send.at[4 + 3 * turn + n], sibling)
                relay.wait_recv()
                relay.start()
        for i in range(4):
            for row in range(NY):
                key_copy(row * NZ + 2 * i + 1 - c, r_send.at[0], sibling).wait_recv()
        for turn in range(4):
            key_copy(0, f_send.at[turn], partner).wait_send()
        for n in range(16):
            key_copy(0, r_send.at[n], sibling).wait_send()

    @pl.when(passing)
    def _():
        for turn in range(4):
            for copy in passed(turn)[1]:
                copy.wait_send()

    for d in range(1, 8):
        other = (head + d) % 8
        remote(cols.at[other], cols.at[other], h_send.at[d], h_recv.at[other], sibling).wait_recv()
    for copy in head_outs + column_outs + outs:
        copy.wait_send()
    for to in order[NZ - 1 - FLIGHT :]:
        send_piece(to, False)


def spread(t_shift, s_shift, tq, tk, tv, hidden, wq, wk, wv):
    anywhere = pl.BlockSpec(memory_space=pl.ANY)
    smem = pl.BlockSpec(memory_space=pltpu.SMEM)
    dma = pltpu.SemaphoreType.DMA
    return pl.pallas_call(
        spread_kernel,
        name="spread",
        out_shape=(
            jax.ShapeDtypeStruct((SLOTS, PIECE, 128), BF16),
            jax.ShapeDtypeStruct((8, 4, 64, TOK), BF16),
        ),
        in_specs=[smem, smem] + [anywhere] * 7,
        out_specs=(anywhere, anywhere),
        scratch_shapes=[
            pltpu.VMEM((PAIRS, TOK, 512), BF16),
            pltpu.VMEM((TOK, 2048), BF16),
            pltpu.VMEM((2048, 384), BF16),
            pltpu.VMEM((3 * TOK, 256), BF16),
            pltpu.VMEM((3 * TOK, 256), BF16),
            pltpu.VMEM((3 * TOK, 128), BF16),
            pltpu.VMEM((NZ, PIECE, 128), BF16),
            pltpu.VMEM((4, PIECE, 128), BF16),
            pltpu.VMEM((4, 128, TOK), BF16),
            dma((10,)), dma((4,)), dma((4,)), dma((4,)), dma((4,)),
            dma((NZ,)), dma((SLOTS,)), dma((4,)), dma((4,)), dma((8,)), dma((16,)),
            dma((4,)), dma((4,)), dma((8,)), dma((8,)),
        ],
        compiler_params=pltpu.CompilerParams(
            collective_id=0, has_side_effects=True, vmem_limit_bytes=VMEM_LIMIT
        ),
    )(t_shift, s_shift, tq, tk, tv, hidden, wq, wk, wv)


def in_three(row):
    high = row.astype(BF16).astype(F32)
    middle = (row - high).astype(BF16).astype(F32)
    low = row - high - middle
    at = lax.broadcasted_iota(jnp.int32, (16, 128), 0)
    tile = jnp.where(at == 0, high, jnp.where(at == 1, middle, jnp.where(at == 2, low, jnp.float32(0.0))))
    return tile.astype(BF16)


def relate_kernel(lengths, keys, part, kt, kst, ks, st, ss, acc, load):
    _, _, y, z, _, c = place()
    group = 2 * (y % 2) + c
    coef = jnp.float32(1.0 / 48.0)
    scale = jnp.float32(1.0 / 16.0)
    scale2 = jnp.float32(math.log2(math.e) / 16.0)
    two = ROWS // TOK
    blocks = KEYS // ROWS
    last_dims = (((1,), (1,)), ((), ()))

    @pl.when(pair_at(z, y // 2) < PAIRS)
    def _():
        loads = [
            pltpu.make_async_copy(keys.at[:, 256:320], kst, load.at[2]),
            pltpu.make_async_copy(keys.at[:, 0:128], kt.at[:, :, 0:128], load.at[0]),
            pltpu.make_async_copy(keys.at[:, 128:256], kt.at[:, :, 128:256], load.at[1]),
        ]
        for copy in loads:
            copy.start()
        acc[...] = jnp.zeros_like(acc)
        end0 = lengths[0]
        end1 = end0 + lengths[1]
        end2 = end1 + lengths[2]

        def first_of(position):
            zero = jnp.int32(0)
            start = jnp.where(position >= end0, end0, zero)
            start = jnp.where(position >= end1, end1, start)
            return jnp.where(position >= end2, end2, start)

        most = jnp.maximum(jnp.maximum(lengths[0], lengths[1]), jnp.maximum(lengths[2], lengths[3]))
        last = jnp.where(
            lengths[0] == most, end0, jnp.where(lengths[1] == most, end1, jnp.where(lengths[2] == most, end2, KEYS))
        )
        last_block = (last - 1) // ROWS
        unit = jnp.where(
            lax.broadcasted_iota(jnp.int32, (TOK, TOK), 0) == lax.broadcasted_iota(jnp.int32, (TOK, TOK), 1),
            jnp.float32(1.0),
            jnp.float32(0.0),
        ).astype(BF16)
        loads[0].wait()

        @pl.loop(0, SLOTS // 8)
        def _(n):
            for u in range(8):
                ks[8 * n + u] = lax.dot_general(
                    unit, kst[8 * n + u], last_dims, preferred_element_type=F32
                ).astype(BF16)

        for copy in loads[1:]:
            copy.wait()

        def one_block(t, div):
            falling = jnp.logical_or(t == 1, t == 2)
            nth = 4 * t + jnp.where(falling, 3 - group, group)
            block = (last_block + blocks - nth) % blocks
            r0 = block * ROWS
            lower = first_of(r0) // ROWS
            upper = block + 1
            latest = first_of(r0 + ROWS - 1)
            row = r0 + lax.broadcasted_iota(jnp.int32, (8, ROWS), 1)
            start = first_of(row)
            sub_row = lax.broadcasted_iota(jnp.int32, (8, ROWS), 0)
            bt = jnp.concatenate([kst[block * two + u] for u in range(two)], axis=1)
            b2 = (bt.astype(F32) * jnp.float32(2.0)).astype(BF16)

            def online(n, carry, width, mask):
                mt, ms, tot_t, tot_s, cross = carry
                k0 = pl.multiple_of(n * ROWS, ROWS)
                slots = pl.ds(n * two, width // TOK)
                a = lax.dot_general(
                    kt[slots].reshape(width, 256),
                    kt[pl.ds(block * two, two)].reshape(ROWS, 256),
                    last_dims,
                    preferred_element_type=F32,
                )
                b = jnp.dot(ks[slots].reshape(width, 64), b2, preferred_element_type=F32)
                for first in range(0, width, 64):
                    xs, ws = [], []
                    new_t, new_s = mt, ms
                    for g in range(first, first + 64, 8):
                        x = a[g : g + 8]
                        w = b[g : g + 8]
                        if mask:
                            column = sub_row + (k0 + g)
                            allowed = jnp.logical_and(column >= start, column <= row)
                            x = jnp.where(allowed, x, NEG)
                            w = jnp.where(allowed, w, NEG)
                        st[pl.ds(pl.multiple_of(k0 + g, 8), 8)] = x
                        ss[pl.ds(pl.multiple_of(k0 + g, 8), 8)] = w
                        new_t = jnp.maximum(new_t, x)
                        new_s = jnp.maximum(new_s, w)
                        xs.append(x)
                        ws.append(w)
                    fade = jnp.exp2((mt - new_t) * scale2)
                    tot_t = tot_t * fade
                    cross = cross * fade
                    tot_s = tot_s * jnp.exp2((ms - new_s) * scale2)
                    mt, ms = new_t, new_s
                    for x, w in zip(xs, ws):
                        ea = jnp.exp2((x - mt) * scale2)
                        tot_t = tot_t + ea
                        tot_s = tot_s + jnp.exp2((w - ms) * scale2)
                        cross = cross + ea * (x - w)
                return mt, ms, tot_t, tot_s, cross

            inner = jnp.minimum((latest + ROWS - 1) // ROWS, upper)
            wide = (jnp.maximum(block, inner) - inner) // 2
            narrow = upper - lower - 2 * wide

            def nth_narrow(n):
                return jnp.where(lower + n < inner, lower + n, lower + n + 2 * wide)

            low = jnp.full((8, ROWS), NEG, F32)
            zero = jnp.zeros((8, ROWS), F32)
            carry = lax.fori_loop(
                0, narrow, lambda n, carry: online(nth_narrow(n), carry, ROWS, True), (low, low, zero, zero, zero)
            )
            mt, ms, tot_t, tot_s, cross = lax.fori_loop(
                0, wide, lambda n, carry: online(inner + 2 * n, carry, CHUNK, False), carry
            )
            top_t = jnp.max(mt, axis=0, keepdims=True)
            top_s = jnp.max(ms, axis=0, keepdims=True)
            fade = jnp.exp2((mt - top_t) * scale2)
            tot_t = jnp.sum(tot_t * fade, axis=0, keepdims=True)
            tot_s = jnp.sum(tot_s * jnp.exp2((ms - top_s) * scale2), axis=0, keepdims=True)
            mixed = jnp.sum(cross * fade, axis=0, keepdims=True)
            value = (mixed / tot_t + (top_s - top_t)) * scale + (jnp.log(tot_s) - jnp.log(tot_t))
            div = div + value[:, 0:128] + value[:, 128:256]
            log_t = jnp.log2(coef / tot_t)
            log_s = jnp.log2(coef / tot_s)

            def gradient(n, near, width):
                k0 = pl.multiple_of(n * ROWS, ROWS)
                pieces = []
                for g in range(0, width, 64):
                    at = pl.ds(pl.multiple_of(k0 + g, 64), 64)
                    pieces.append(
                        (
                            jnp.exp2((ss[at] - top_s) * scale2 + log_s)
                            - jnp.exp2((st[at] - top_t) * scale2 + log_t)
                        ).astype(BF16)
                    )
                g = jnp.concatenate(pieces, axis=0)
                columns = jnp.concatenate([kst[n * two + u] for u in range(width // TOK)], axis=1)
                acc[:, pl.ds(k0, width)] += lax.dot_general(bt, g, last_dims, preferred_element_type=F32)
                return near + jnp.dot(columns, g, preferred_element_type=F32)

            near = lax.fori_loop(
                0, narrow, lambda n, near: gradient(nth_narrow(n), near, ROWS), jnp.zeros((64, ROWS), F32)
            )
            near = lax.fori_loop(0, wide, lambda n, near: gradient(inner + 2 * n, near, CHUNK), near)
            acc[:, pl.ds(pl.multiple_of(r0, ROWS), ROWS)] += near
            return div

        div = lax.fori_loop(0, 4, one_block, jnp.zeros((1, 128), F32))
        tile = in_three(div)
        for row in range(NY):
            for parity in range(2):
                for i in range(4):
                    base = (row * NZ + 2 * i + parity) * TOK
                    part[parity, row, i * 64 : (i + 1) * 64] = (
                        acc[:, base : base + TOK] * jnp.float32(1.0 / 8.0)
                    ).astype(BF16)
                part[parity, row, 256:PART] = tile


def relate(lengths, keys):
    vmem = pl.BlockSpec(memory_space=pltpu.VMEM)
    smem = pl.BlockSpec(memory_space=pltpu.SMEM)
    return pl.pallas_call(
        relate_kernel,
        name="relate",
        out_shape=jax.ShapeDtypeStruct((2, NY, PART, 128), BF16),
        in_specs=[smem, pl.BlockSpec(memory_space=pl.ANY)],
        out_specs=vmem,
        scratch_shapes=[
            pltpu.VMEM((SLOTS, TOK, 256), BF16),
            pltpu.VMEM((SLOTS, 64, TOK), BF16),
            pltpu.VMEM((SLOTS, TOK, 64), BF16),
            pltpu.VMEM((KEYS, ROWS), F32),
            pltpu.VMEM((KEYS, ROWS), F32),
            pltpu.VMEM((64, KEYS), F32),
            pltpu.SemaphoreType.DMA((3,)),
        ],
        compiler_params=pltpu.CompilerParams(vmem_limit_bytes=VMEM_LIMIT),
    )(lengths, keys)


def fold_kernel(
    part, cols, mean, both,
    own, in0, pre, in1, sums, in2, outp, in4, win, prev, follow, div_x, div_1, fetched,
    load, l0, s0, r0, s1, r1, s2, r2, s4, r4, sw, rw, sv, rv, sx, rx,
):
    seq, head, y, z, x, c = place()
    ahead = (seq, (head + 1) % 8)
    behind = (seq, (head + 7) % 8)
    other = head + 1 - 2 * c
    fetch = pltpu.make_async_copy(cols, fetched, load)
    fetch.start()
    active = pair_at(z, y // 2) < PAIRS
    mine = pltpu.make_async_copy(part.at[c], own, l0)

    @pl.when(active)
    def _():
        mine.start()

    peers = [(seq, (head + d) % 8) for d in range(1, 8)]
    for dz in range(1, NZ):
        for h in (head, other):
            peers.append((y * NZ + (z + dz) % NZ, h))
    for dy in range(1, NY):
        peers.append((((y + dy) % NY) * NZ + z, head))
        peers.append((((y + dy) % NY) * NZ + z + 1 - 2 * (z % 2), head))
    greet(peers)()
    across = remote(part.at[1 - c], in0, s0, r0, (seq, other))
    row_copies = [
        remote(pre.at[(y + dy) % NY], in1.at[y], s1.at[dy], r1.at[y], (((y + dy) % NY) * NZ + z, head))
        for dy in (2, 1, 3)
    ]

    @pl.when(active)
    def _():
        across.start()
        mine.wait()
        across.wait_recv()
        for turn in range(NY):
            row = (y + (2, 1, 3, 0)[turn]) % NY
            pre[row, 0:256] = (own[row, 0:256].astype(F32) + in0[row, 0:256].astype(F32)).astype(BF16)
            tiles = own[row, 256:PART].astype(F32) + in0[row, 256:PART].astype(F32)
            pre[row, 256:PART] = in_three(jnp.sum(tiles, axis=0, keepdims=True))
            if turn < 3:
                row_copies[turn].start()
            else:
                pltpu.make_async_copy(pre.at[y], in1.at[y], r1.at[y]).start()

    def each_pair_copy(p, go):
        k = pair_at(z, p)
        for turn in (2, 1, 3, 0):
            to = (z // 2 + turn) % 4 * 2 + c
            copy = remote(sums.at[p], in2.at[k], s2.at[p * 4 + turn], r2.at[k], (y * NZ + to, 2 * x + p))
            mine = jnp.logical_and(c == p, z == to)

            @pl.when(jnp.logical_not(mine))
            def _():
                copy.start() if go else copy.wait_send()

            if go:
                @pl.when(mine)
                def _():
                    pltpu.make_async_copy(sums.at[p], in2.at[k], r2.at[k]).start()

    for p in range(2):
        @pl.when(pair_at(z, p) < PAIRS)
        def _():
            total = jnp.zeros((256, 128), F32)
            tiles = jnp.zeros((16, 128), F32)
            for n in range(2 * p, 2 * p + 2):
                pltpu.make_async_copy(in1.at[n], in1.at[n], r1.at[n]).wait()
                total = total + in1[n, 0:256].astype(F32)
                tiles = tiles + in1[n, 256:PART].astype(F32)
            sums[p, 0:256] = total.astype(BF16)
            sums[p, 256:PART] = in_three(jnp.sum(tiles, axis=0, keepdims=True))
            each_pair_copy(p, True)

    fetch.wait()
    tiles = jnp.zeros((16, 128), F32)
    for k in range(PAIRS):
        pltpu.make_async_copy(in2.at[k], in2.at[k], r2.at[k]).wait()
    for k in range(PAIRS):
        tiles = tiles + in2[k, 256:PART].astype(F32)
    grad = jnp.zeros((512, 384), F32)
    for i in range(4):
        grad = grad + lax.dot_general(
            fetched[:, i].reshape(512, TOK), in2[0:PAIRS, i * 64 : (i + 1) * 64].reshape(384, TOK),
            (((1,), (1,)), ((), ())),
            preferred_element_type=F32,
        )
    for n in range(8):
        outp[n] = grad[n * 64 : (n + 1) * 64].astype(BF16)

    slot = y * 2 + z % 2
    block_copies = []
    for d in (4, 5, 2, 3, 6, 7, 1):
        to = (slot + d) % 8
        block_copies.append(
            remote(
                outp.at[to], in4.at[slot], s4.at[d], r4.at[slot],
                ((to // 2) * NZ + (z // 2) * 2 + to % 2, head),
            )
        )
    for copy in block_copies:
        copy.start()
    pltpu.make_async_copy(outp.at[slot], in4.at[slot], r4.at[slot]).start()

    div_1[...] = jnp.broadcast_to(jnp.sum(tiles, axis=0, keepdims=True), (8, 128))
    pltpu.make_async_copy(div_1, div_x.at[head], rx.at[head]).start()
    div_copies = [remote(div_1, div_x.at[head], sx.at[d], rx.at[head], (seq, (head + d) % 8)) for d in range(1, 8)]
    for copy in div_copies:
        copy.start()

    total = jnp.zeros((64, 384), F32)
    for n in range(8):
        pltpu.make_async_copy(in4.at[n], in4.at[n], r4.at[n]).wait()
        total = total + in4[n].astype(F32)
    win[...] = total.astype(BF16)
    lasts = [remote(win, prev, sw, rw, ahead), remote(win, follow, sv, rv, behind)]
    for copy in lasts:
        copy.start()
    both[:, 384:768] = win[...]
    for copy in block_copies + div_copies:
        copy.wait_send()

    @pl.when(active)
    def _():
        across.wait_send()
        for copy in row_copies:
            copy.wait_send()

    for p in range(2):
        @pl.when(pair_at(z, p) < PAIRS)
        def _():
            each_pair_copy(p, False)

    total = jnp.zeros((8, 128), F32)
    for n in range(8):
        pltpu.make_async_copy(div_x.at[n], div_x.at[n], rx.at[n]).wait()
        total = total + div_x[n]
    mean[0, 0] = jnp.sum(total[0:1]) * jnp.float32(1.0 / 196608.0)
    for copy in lasts:
        copy.wait_send()
        copy.wait_recv()
    both[:, 0:384] = prev[...]
    both[:, 768:1152] = follow[...]


def fold(part, cols):
    vmem = pl.BlockSpec(memory_space=pltpu.VMEM)
    smem = pl.BlockSpec(memory_space=pltpu.SMEM)
    dma = pltpu.SemaphoreType.DMA
    return pl.pallas_call(
        fold_kernel,
        name="fold",
        out_shape=(jax.ShapeDtypeStruct((1, 1), F32), jax.ShapeDtypeStruct((64, 1152), BF16)),
        in_specs=[pl.BlockSpec(memory_space=pl.ANY)] * 2,
        out_specs=(smem, vmem),
        scratch_shapes=[
            pltpu.VMEM((NY, PART, 128), BF16),
            pltpu.VMEM((NY, PART, 128), BF16),
            pltpu.VMEM((NY, PART, 128), BF16),
            pltpu.VMEM((NY, PART, 128), BF16),
            pltpu.VMEM((2, PART, 128), BF16),
            pltpu.VMEM((NZ, PART, 128), BF16),
            pltpu.VMEM((8, 64, 384), BF16),
            pltpu.VMEM((8, 64, 384), BF16),
            pltpu.VMEM((64, 384), BF16),
            pltpu.VMEM((64, 384), BF16),
            pltpu.VMEM((64, 384), BF16),
            pltpu.VMEM((8, 8, 128), F32),
            pltpu.VMEM((8, 128), F32),
            pltpu.VMEM((8, 4, 64, TOK), BF16),
            dma(()), dma(()), dma(()), dma(()), dma((NY,)), dma((NY,)), dma((8,)), dma((NZ,)), dma((8,)), dma((8,)),
            dma(()), dma(()), dma(()), dma(()), dma((8,)), dma((8,)),
        ],
        compiler_params=pltpu.CompilerParams(
            collective_id=1, has_side_effects=True, vmem_limit_bytes=VMEM_LIMIT
        ),
    )(part, cols)


def shift_kernel(s_shift, both, gq, gk, gv):
    there = lax.broadcasted_iota(jnp.int32, (384, 128), 0)
    here = lax.broadcasted_iota(jnp.int32, (384, 128), 1)
    pick = jnp.where(there == here + (192 - s_shift[0]), jnp.float32(1.0), jnp.float32(0.0)).astype(BF16)
    for kind, out in enumerate((gq, gk, gv)):
        out[...] = functools.reduce(
            jnp.add,
            [
                jnp.dot(
                    both[:, 384 * n + 128 * kind : 384 * n + 128 * kind + 128],
                    pick[128 * n : 128 * n + 128],
                    preferred_element_type=F32,
                )
                for n in range(3)
            ],
        ).astype(BF16)


def shift(s_shift, both):
    vmem = pl.BlockSpec(memory_space=pltpu.VMEM)
    grad = jax.ShapeDtypeStruct((64, 128), BF16)
    return pl.pallas_call(
        shift_kernel,
        name="shift",
        out_shape=(grad, grad, grad),
        in_specs=[pl.BlockSpec(memory_space=pltpu.SMEM), vmem],
        out_specs=(vmem, vmem, vmem),
    )(s_shift, both)


def local(
    teacher_query, teacher_key, teacher_value, student_hidden, weight_query, weight_key, weight_value,
    teacher_shift, student_shift, segment_lengths,
):
    keys, cols = spread(
        teacher_shift, student_shift, teacher_query, teacher_key, teacher_value, student_hidden,
        weight_query, weight_key, weight_value,
    )
    mean, both = fold(relate(segment_lengths, keys), cols)
    return (mean[0, 0], *shift(student_shift, both))


def solution(mesh):
    in_specs = (
        P("seq", "head"),
        P("seq", "head"),
        P("seq", "head"),
        P("seq", None),
        P(None, "head"),
        P(None, "head"),
        P(None, "head"),
        P(),
        P(),
        P(),
    )
    out_specs = (P(), P("seq", "head"), P("seq", "head"), P("seq", "head"))
    return jax.shard_map(local, mesh=mesh, in_specs=in_specs, out_specs=out_specs, check_vma=False)
```

```python
import functools
import math

import jax
import jax.numpy as jnp
from jax import lax
from jax.experimental import pallas as pl
from jax.experimental.pallas import tpu as pltpu
from jax.sharding import PartitionSpec as P

MESH = pl.DeviceIdType.MESH
NEG = -1e30
TOK = 128
NZ = 8
NY = 4
PAIRS = 6
VMEM_LIMIT = 60 * 1024 * 1024
SLOTS = NY * NZ
PIECE = 320
ROWS = 256
CHUNK = 512
FLIGHT = 2
PART = 272
KEYS = SLOTS * TOK
F32 = jnp.float32
BF16 = jnp.bfloat16


def place():
    seq = lax.axis_index("seq")
    head = lax.axis_index("head")
    return seq, head, seq // NZ, seq % NZ, head // 2, head % 2


def pair_at(z, group):
    return (z + 4 * group) % NZ


def greet(peers):
    barrier = pltpu.get_barrier_semaphore()
    for peer in peers:
        pl.semaphore_signal(barrier, inc=1, device_id=peer, device_id_type=MESH)
    return lambda: pl.semaphore_wait(barrier, len(peers))


def remote(src, dst, send, recv, device):
    return pltpu.make_async_remote_copy(
        src_ref=src, dst_ref=dst, send_sem=send, recv_sem=recv, device_id=device, device_id_type=MESH
    )


def spread_kernel(
    t_shift, s_shift, tq, tk, tv, hidden, wq, wk, wv,
    keys, cols,
    stack, tokens, weights, small_n, small_p, stud, piece, transit, hid,
    load, n_send, n_recv, p_send, p_recv,
    k_send, key_sem, tr_sem, f_send, g_send, r_send, z_send, z_recv, h_send, h_recv,
):
    seq, head, y, z, x, c = place()
    sibling = (seq, head + 1 - 2 * c)
    behind = (seq, (head + 7) % 8)
    teachers = (tq, tk, tv)
    loads = [pltpu.make_async_copy(hidden, tokens, load.at[0])]
    for kind, weight in enumerate((wq, wk, wv)):
        loads.append(pltpu.make_async_copy(weight, weights.at[kind], load.at[1 + kind]))
    for kind in range(3):
        for j in range(2):
            loads.append(
                pltpu.make_async_copy(
                    teachers[kind].at[:, 128 * j : 128 * j + 384],
                    stack.at[2 * kind + j, :, 128 - 128 * j : 512 - 128 * j],
                    load.at[4 + 2 * kind + j],
                )
            )
    for copy in loads:
        copy.start()

    peers = [(seq, (head + d) % 8) for d in range(1, 8)]
    for dz in range(1, NZ):
        other = y * NZ + (z + dz) % NZ
        peers.append((other, head))
        peers.append((other, sibling[1]))
    for dy in range(1, NY):
        peers.append((((y + dy) % NY) * NZ + z, head))
    wait_all = greet(peers)

    loads[0].wait()
    for kind in range(3):
        loads[1 + kind].wait()
        stud[:, kind * 128 : (kind + 1) * 128] = jnp.dot(
            tokens[...], weights[kind], preferred_element_type=F32
        ).astype(BF16)
    wait_all()

    ahead = (seq, (head + 1) % 8)
    outs = []
    for kind in range(3):
        first, last = teachers[kind].at[:, 0:128], teachers[kind].at[:, 384:512]
        outs.append(
            remote(first, stack.at[2 * kind + 1, :, 384:512], n_send.at[kind], n_recv.at[kind], behind)
        )
        outs.append(remote(last, stack.at[2 * kind, :, 0:128], p_send.at[kind], p_recv.at[kind], ahead))
    outs.append(remote(stud, small_n, n_send.at[3], n_recv.at[3], behind))
    outs.append(remote(stud, small_p, p_send.at[3], p_recv.at[3], ahead))
    for copy in outs[6:] + outs[:6]:
        copy.start()

    for part in range(4):
        first = pl.multiple_of(head // 2 * 512 + part * 128, 128)
        hid[part] = jnp.transpose(tokens[:, pl.ds(first, 128)].astype(F32)).astype(BF16)
    mine = pl.ds(pl.multiple_of(c * 64, 64), 64)
    column_outs = []
    for d in range(1, 4):
        to = (z + 2 * d) % NZ
        column_outs.append(
            remote(
                hid.at[to // 2, mine], cols.at[head, z // 2], z_send.at[d], z_recv.at[z // 2], (y * NZ + to, head)
            )
        )
    for copy in column_outs:
        copy.start()
    pltpu.make_async_copy(hid.at[z // 2, mine], cols.at[head, z // 2], z_recv.at[z // 2]).start()

    def one_hot(rows, columns, first, dim):
        there = lax.broadcasted_iota(jnp.int32, (rows, columns), dim)
        here = lax.broadcasted_iota(jnp.int32, (rows, columns), 1 - dim)
        return jnp.where(there == here + first, jnp.float32(1.0), jnp.float32(0.0)).astype(BF16)

    pick_t = one_hot(512, 256, t_shift[0] - 128, 0)
    pick_s = (one_hot(64, 256, s_shift[0] + 64, 1), one_hot(64, 256, s_shift[0], 1))
    own_pair = c == y // 2
    core = z % 2

    def send_piece(to, go):
        k = pair_at(to, c)
        target = (y * NZ + to, 2 * x + core)
        some = k < PAIRS
        here = jnp.logical_and(some, jnp.logical_and(z == to, core == c))
        there = jnp.logical_and(some, jnp.logical_not(here))

        @pl.when(jnp.logical_and(own_pair, there))
        def _():
            copy = remote(piece.at[k], keys.at[seq], k_send.at[k], key_sem.at[seq], target)
            copy.start() if go else copy.wait_send()

        @pl.when(jnp.logical_and(jnp.logical_not(own_pair), there))
        def _():
            copy = remote(piece.at[k], transit.at[z // 2], k_send.at[k], tr_sem.at[z // 2], target)
            copy.start() if go else copy.wait_send()

        if go:
            @pl.when(jnp.logical_and(own_pair, here))
            def _():
                pltpu.make_async_copy(piece.at[k], keys.at[seq], key_sem.at[seq]).start()

            @pl.when(jnp.logical_and(jnp.logical_not(own_pair), here))
            def _():
                pltpu.make_async_copy(piece.at[k], transit.at[z // 2], tr_sem.at[z // 2]).start()

    transposed = (((1,), (1,)), ((), ()))
    for copy in outs[6:]:
        copy.wait_recv()
    for k in range(PAIRS):
        at = slice(k // 2 * 128, (k // 2 + 1) * 128)
        before, after = (small_p, stud) if k % 2 == 0 else (stud, small_n)
        pick = pick_s[k % 2]
        small = lax.dot_general(
            pick[:, 0:128], before[:, at], transposed, preferred_element_type=F32
        ) + lax.dot_general(pick[:, 128:256], after[:, at], transposed, preferred_element_type=F32)
        piece[k, 256:320] = small.astype(BF16)
    for copy in loads[4:]:
        copy.wait()
    for copy in outs[:6]:
        copy.wait_recv()
    window = jnp.dot(stack[...].reshape(PAIRS * TOK, 512), pick_t, preferred_element_type=F32)
    for k in range(PAIRS):
        piece[k, 0:128] = window[k * TOK : (k + 1) * TOK, 0:128].astype(BF16)
        piece[k, 128:256] = window[k * TOK : (k + 1) * TOK, 128:256].astype(BF16)
    order = [(z + d + NZ) % NZ for d in (0, 1, -1, 2, -2, 3, -3, 4)]
    for n, to in enumerate(order):
        if n > FLIGHT:
            send_piece(order[n - 1 - FLIGHT], False)
        send_piece(to, True)

    active = pair_at(z, y // 2) < PAIRS
    passing = pair_at(z, 1 - y // 2) < PAIRS
    beside = y + 1 - 2 * (y % 2)
    partner = (beside * NZ + z, head)
    opposite = ((3 - y) * NZ + z, head)

    def key_copy(slot, send, device):
        return remote(keys.at[slot], keys.at[slot], send, key_sem.at[slot], device)

    def source(turn):
        same = (0, 2, 6, 4)[turn]
        cross = (1, 7, 3, 5)[turn]
        return (z + jnp.where(core == c, same, cross)) % NZ

    def forwards(turn):
        slot = y * NZ + source(turn)
        return key_copy(slot, f_send.at[turn], partner), key_copy(slot, r_send.at[turn], sibling)

    def passed(turn):
        slot = y * NZ + source(turn)
        i = source(turn) // 2
        return i, [
            remote(
                transit.at[i], keys.at[slot], g_send.at[2 * turn + n], key_sem.at[slot],
                ((row * NZ) + z, head),
            )
            for n, row in enumerate((3 - y, 3 - beside))
        ]

    for turn in range(4):
        @pl.when(passing)
        def _():
            i, copies = passed(turn)
            remote(transit.at[i], transit.at[i], g_send.at[2 * turn], tr_sem.at[i], partner).wait_recv()
            for copy in copies:
                copy.start()

        @pl.when(active)
        def _():
            first, relay = forwards(turn)
            first.wait_recv()
            first.start()
            relay.start()

    for i in range(4):
        pltpu.make_async_copy(hid.at[i, mine], cols.at[head, i], z_recv.at[i]).wait()
    head_outs = []
    for d in range(1, 8):
        head_outs.append(
            remote(cols.at[head], cols.at[head], h_send.at[d], h_recv.at[head], (seq, (head + d) % 8))
        )
    for copy in head_outs:
        copy.start()

    @pl.when(active)
    def _():
        for turn in range(4):
            for n, row in enumerate((beside, 3 - y, 3 - beside)):
                relay = key_copy(row * NZ + source(turn), r_send.at[4 + 3 * turn + n], sibling)
                relay.wait_recv()
                relay.start()
        for i in range(4):
            for row in range(NY):
                key_copy(row * NZ + 2 * i + 1 - c, r_send.at[0], sibling).wait_recv()
        for turn in range(4):
            key_copy(0, f_send.at[turn], partner).wait_send()
        for n in range(16):
            key_copy(0, r_send.at[n], sibling).wait_send()

    @pl.when(passing)
    def _():
        for turn in range(4):
            for copy in passed(turn)[1]:
                copy.wait_send()

    for d in range(1, 8):
        other = (head + d) % 8
        remote(cols.at[other], cols.at[other], h_send.at[d], h_recv.at[other], sibling).wait_recv()
    for copy in head_outs + column_outs + outs:
        copy.wait_send()
    for to in order[NZ - 1 - FLIGHT :]:
        send_piece(to, False)


def spread(t_shift, s_shift, tq, tk, tv, hidden, wq, wk, wv):
    anywhere = pl.BlockSpec(memory_space=pl.ANY)
    smem = pl.BlockSpec(memory_space=pltpu.SMEM)
    dma = pltpu.SemaphoreType.DMA
    return pl.pallas_call(
        spread_kernel,
        name="spread",
        out_shape=(
            jax.ShapeDtypeStruct((SLOTS, PIECE, 128), BF16),
            jax.ShapeDtypeStruct((8, 4, 64, TOK), BF16),
        ),
        in_specs=[smem, smem] + [anywhere] * 7,
        out_specs=(anywhere, anywhere),
        scratch_shapes=[
            pltpu.VMEM((PAIRS, TOK, 512), BF16),
            pltpu.VMEM((TOK, 2048), BF16),
            pltpu.VMEM((3, 2048, 128), BF16),
            pltpu.VMEM((TOK, 384), BF16),
            pltpu.VMEM((TOK, 384), BF16),
            pltpu.VMEM((TOK, 384), BF16),
            pltpu.VMEM((NZ, PIECE, 128), BF16),
            pltpu.VMEM((4, PIECE, 128), BF16),
            pltpu.VMEM((4, 128, TOK), BF16),
            dma((10,)), dma((4,)), dma((4,)), dma((4,)), dma((4,)),
            dma((NZ,)), dma((SLOTS,)), dma((4,)), dma((4,)), dma((8,)), dma((16,)),
            dma((4,)), dma((4,)), dma((8,)), dma((8,)),
        ],
        compiler_params=pltpu.CompilerParams(
            collective_id=0, has_side_effects=True, vmem_limit_bytes=VMEM_LIMIT
        ),
    )(t_shift, s_shift, tq, tk, tv, hidden, wq, wk, wv)


def in_three(row):
    high = row.astype(BF16).astype(F32)
    middle = (row - high).astype(BF16).astype(F32)
    low = row - high - middle
    at = lax.broadcasted_iota(jnp.int32, (16, 128), 0)
    tile = jnp.where(at == 0, high, jnp.where(at == 1, middle, jnp.where(at == 2, low, jnp.float32(0.0))))
    return tile.astype(BF16)


def relate_kernel(lengths, keys, part, kt, kst, ks, st, ss, acc, load):
    _, _, y, z, _, c = place()
    group = 2 * (y % 2) + c
    coef = jnp.float32(1.0 / 48.0)
    scale = jnp.float32(1.0 / 16.0)
    scale2 = jnp.float32(math.log2(math.e) / 16.0)
    two = ROWS // TOK
    blocks = KEYS // ROWS
    last_dims = (((1,), (1,)), ((), ()))

    @pl.when(pair_at(z, y // 2) < PAIRS)
    def _():
        loads = [
            pltpu.make_async_copy(keys.at[:, 256:320], kst, load.at[2]),
            pltpu.make_async_copy(keys.at[:, 0:128], kt.at[:, :, 0:128], load.at[0]),
            pltpu.make_async_copy(keys.at[:, 128:256], kt.at[:, :, 128:256], load.at[1]),
        ]
        for copy in loads:
            copy.start()
        acc[...] = jnp.zeros_like(acc)
        end0 = lengths[0]
        end1 = end0 + lengths[1]
        end2 = end1 + lengths[2]

        def first_of(position):
            zero = jnp.int32(0)
            start = jnp.where(position >= end0, end0, zero)
            start = jnp.where(position >= end1, end1, start)
            return jnp.where(position >= end2, end2, start)

        most = jnp.maximum(jnp.maximum(lengths[0], lengths[1]), jnp.maximum(lengths[2], lengths[3]))
        last = jnp.where(
            lengths[0] == most, end0, jnp.where(lengths[1] == most, end1, jnp.where(lengths[2] == most, end2, KEYS))
        )
        last_block = (last - 1) // ROWS
        unit = jnp.where(
            lax.broadcasted_iota(jnp.int32, (TOK, TOK), 0) == lax.broadcasted_iota(jnp.int32, (TOK, TOK), 1),
            jnp.float32(1.0),
            jnp.float32(0.0),
        ).astype(BF16)
        loads[0].wait()

        @pl.loop(0, SLOTS // 8)
        def _(n):
            for u in range(8):
                ks[8 * n + u] = lax.dot_general(
                    unit, kst[8 * n + u], last_dims, preferred_element_type=F32
                ).astype(BF16)

        for copy in loads[1:]:
            copy.wait()

        def one_block(t, div):
            odd = t % 2
            nth = 4 * t + odd * 3 + (1 - 2 * odd) * group
            block = (last_block + blocks - nth) % blocks
            r0 = block * ROWS
            lower = first_of(r0) // ROWS
            upper = block + 1
            latest = first_of(r0 + ROWS - 1)
            row = r0 + lax.broadcasted_iota(jnp.int32, (8, ROWS), 1)
            start = first_of(row)
            sub_row = lax.broadcasted_iota(jnp.int32, (8, ROWS), 0)
            bt = jnp.concatenate([kst[block * two + u] for u in range(two)], axis=1)
            b2 = (bt.astype(F32) * jnp.float32(2.0)).astype(BF16)

            def online(n, carry, width, mask):
                mt, ms, tot_t, tot_s, cross = carry
                k0 = pl.multiple_of(n * ROWS, ROWS)
                slots = pl.ds(n * two, width // TOK)
                a = lax.dot_general(
                    kt[slots].reshape(width, 256),
                    kt[pl.ds(block * two, two)].reshape(ROWS, 256),
                    last_dims,
                    preferred_element_type=F32,
                )
                b = jnp.dot(ks[slots].reshape(width, 64), b2, preferred_element_type=F32)
                for first in range(0, width, 64):
                    xs, ws = [], []
                    new_t, new_s = mt, ms
                    for g in range(first, first + 64, 8):
                        x = a[g : g + 8]
                        w = b[g : g + 8]
                        if mask:
                            column = sub_row + (k0 + g)
                            allowed = jnp.logical_and(column >= start, column <= row)
                            x = jnp.where(allowed, x, NEG)
                            w = jnp.where(allowed, w, NEG)
                        st[pl.ds(pl.multiple_of(k0 + g, 8), 8)] = x
                        ss[pl.ds(pl.multiple_of(k0 + g, 8), 8)] = w
                        new_t = jnp.maximum(new_t, x)
                        new_s = jnp.maximum(new_s, w)
                        xs.append(x)
                        ws.append(w)
                    fade = jnp.exp2((mt - new_t) * scale2)
                    tot_t = tot_t * fade
                    cross = cross * fade
                    tot_s = tot_s * jnp.exp2((ms - new_s) * scale2)
                    mt, ms = new_t, new_s
                    for x, w in zip(xs, ws):
                        ea = jnp.exp2((x - mt) * scale2)
                        tot_t = tot_t + ea
                        tot_s = tot_s + jnp.exp2((w - ms) * scale2)
                        cross = cross + ea * (x - w)
                return mt, ms, tot_t, tot_s, cross

            inner = jnp.minimum((latest + ROWS - 1) // ROWS, upper)
            wide = (jnp.maximum(block, inner) - inner) // 2
            narrow = upper - lower - 2 * wide

            def nth_narrow(n):
                return jnp.where(lower + n < inner, lower + n, lower + n + 2 * wide)

            low = jnp.full((8, ROWS), NEG, F32)
            zero = jnp.zeros((8, ROWS), F32)
            carry = lax.fori_loop(
                0, narrow, lambda n, carry: online(nth_narrow(n), carry, ROWS, True), (low, low, zero, zero, zero)
            )
            mt, ms, tot_t, tot_s, cross = lax.fori_loop(
                0, wide, lambda n, carry: online(inner + 2 * n, carry, CHUNK, False), carry
            )
            top_t = jnp.max(mt, axis=0, keepdims=True)
            top_s = jnp.max(ms, axis=0, keepdims=True)
            fade = jnp.exp2((mt - top_t) * scale2)
            tot_t = jnp.sum(tot_t * fade, axis=0, keepdims=True)
            tot_s = jnp.sum(tot_s * jnp.exp2((ms - top_s) * scale2), axis=0, keepdims=True)
            mixed = jnp.sum(cross * fade, axis=0, keepdims=True)
            value = (mixed / tot_t + (top_s - top_t)) * scale + (jnp.log(tot_s) - jnp.log(tot_t))
            div = div + value[:, 0:128] + value[:, 128:256]
            log_t = jnp.log2(coef / tot_t)
            log_s = jnp.log2(coef / tot_s)

            def gradient(n, near, width):
                k0 = pl.multiple_of(n * ROWS, ROWS)
                pieces = []
                for g in range(0, width, 64):
                    at = pl.ds(pl.multiple_of(k0 + g, 64), 64)
                    pieces.append(
                        (
                            jnp.exp2((ss[at] - top_s) * scale2 + log_s)
                            - jnp.exp2((st[at] - top_t) * scale2 + log_t)
                        ).astype(BF16)
                    )
                g = jnp.concatenate(pieces, axis=0)
                columns = jnp.concatenate([kst[n * two + u] for u in range(width // TOK)], axis=1)
                acc[:, pl.ds(k0, width)] += lax.dot_general(bt, g, last_dims, preferred_element_type=F32)
                return near + jnp.dot(columns, g, preferred_element_type=F32)

            near = lax.fori_loop(
                0, narrow, lambda n, near: gradient(nth_narrow(n), near, ROWS), jnp.zeros((64, ROWS), F32)
            )
            near = lax.fori_loop(0, wide, lambda n, near: gradient(inner + 2 * n, near, CHUNK), near)
            acc[:, pl.ds(pl.multiple_of(r0, ROWS), ROWS)] += near
            return div

        div = lax.fori_loop(0, 4, one_block, jnp.zeros((1, 128), F32))
        tile = in_three(div)
        for row in range(NY):
            for parity in range(2):
                for i in range(4):
                    base = (row * NZ + 2 * i + parity) * TOK
                    part[parity, row, i * 64 : (i + 1) * 64] = (
                        acc[:, base : base + TOK] * jnp.float32(1.0 / 8.0)
                    ).astype(BF16)
                part[parity, row, 256:PART] = tile


def relate(lengths, keys):
    vmem = pl.BlockSpec(memory_space=pltpu.VMEM)
    smem = pl.BlockSpec(memory_space=pltpu.SMEM)
    return pl.pallas_call(
        relate_kernel,
        name="relate",
        out_shape=jax.ShapeDtypeStruct((2, NY, PART, 128), BF16),
        in_specs=[smem, pl.BlockSpec(memory_space=pl.ANY)],
        out_specs=vmem,
        scratch_shapes=[
            pltpu.VMEM((SLOTS, TOK, 256), BF16),
            pltpu.VMEM((SLOTS, 64, TOK), BF16),
            pltpu.VMEM((SLOTS, TOK, 64), BF16),
            pltpu.VMEM((KEYS, ROWS), F32),
            pltpu.VMEM((KEYS, ROWS), F32),
            pltpu.VMEM((64, KEYS), F32),
            pltpu.SemaphoreType.DMA((3,)),
        ],
        compiler_params=pltpu.CompilerParams(vmem_limit_bytes=VMEM_LIMIT),
    )(lengths, keys)


def fold_kernel(
    part, cols, mean, both,
    own, in0, pre, in1, sums, in2, outp, in4, win, prev, follow, div_x, div_1, fetched,
    load, l0, s0, r0, s1, r1, s2, r2, s4, r4, sw, rw, sv, rv, sx, rx,
):
    seq, head, y, z, x, c = place()
    ahead = (seq, (head + 1) % 8)
    behind = (seq, (head + 7) % 8)
    other = head + 1 - 2 * c
    fetch = pltpu.make_async_copy(cols, fetched, load)
    fetch.start()
    active = pair_at(z, y // 2) < PAIRS
    mine = pltpu.make_async_copy(part.at[c], own, l0)

    @pl.when(active)
    def _():
        mine.start()

    peers = [(seq, (head + d) % 8) for d in range(1, 8)]
    for dz in range(1, NZ):
        for h in (head, other):
            peers.append((y * NZ + (z + dz) % NZ, h))
    for dy in range(1, NY):
        peers.append((((y + dy) % NY) * NZ + z, head))
        peers.append((((y + dy) % NY) * NZ + z + 1 - 2 * (z % 2), head))
    greet(peers)()
    across = remote(part.at[1 - c], in0, s0, r0, (seq, other))
    row_copies = [
        remote(pre.at[(y + dy) % NY], in1.at[y], s1.at[dy], r1.at[y], (((y + dy) % NY) * NZ + z, head))
        for dy in (2, 1, 3)
    ]

    @pl.when(active)
    def _():
        across.start()
        mine.wait()
        across.wait_recv()
        for turn in range(NY):
            row = (y + (2, 1, 3, 0)[turn]) % NY
            pre[row, 0:256] = (own[row, 0:256].astype(F32) + in0[row, 0:256].astype(F32)).astype(BF16)
            tiles = own[row, 256:PART].astype(F32) + in0[row, 256:PART].astype(F32)
            pre[row, 256:PART] = in_three(jnp.sum(tiles, axis=0, keepdims=True))
            if turn < 3:
                row_copies[turn].start()
            else:
                pltpu.make_async_copy(pre.at[y], in1.at[y], r1.at[y]).start()

    def each_pair_copy(p, go):
        k = pair_at(z, p)
        for i in range(4):
            copy = remote(sums.at[p], in2.at[k], s2.at[p * 4 + i], r2.at[k], (y * NZ + 2 * i + c, 2 * x + p))
            mine = jnp.logical_and(c == p, z == 2 * i + c)

            @pl.when(jnp.logical_not(mine))
            def _():
                copy.start() if go else copy.wait_send()

            if go:
                @pl.when(mine)
                def _():
                    pltpu.make_async_copy(sums.at[p], in2.at[k], r2.at[k]).start()

    for p in range(2):
        @pl.when(pair_at(z, p) < PAIRS)
        def _():
            total = jnp.zeros((256, 128), F32)
            tiles = jnp.zeros((16, 128), F32)
            for n in range(2 * p, 2 * p + 2):
                pltpu.make_async_copy(in1.at[n], in1.at[n], r1.at[n]).wait()
                total = total + in1[n, 0:256].astype(F32)
                tiles = tiles + in1[n, 256:PART].astype(F32)
            sums[p, 0:256] = total.astype(BF16)
            sums[p, 256:PART] = in_three(jnp.sum(tiles, axis=0, keepdims=True))
            each_pair_copy(p, True)

    fetch.wait()
    tiles = jnp.zeros((16, 128), F32)
    for k in range(PAIRS):
        pltpu.make_async_copy(in2.at[k], in2.at[k], r2.at[k]).wait()
    for k in range(PAIRS):
        tiles = tiles + in2[k, 256:PART].astype(F32)
    slot = y * 2 + z % 2
    block_copies = []
    for turn in (2, 1, 3, 0):
        row = (y + turn) % NY
        grad = jnp.zeros((128, 384), F32)
        for i in range(4):
            grad = grad + lax.dot_general(
                fetched[pl.ds(2 * row, 2), i].reshape(128, TOK),
                in2[0:PAIRS, i * 64 : (i + 1) * 64].reshape(384, TOK),
                (((1,), (1,)), ((), ())),
                preferred_element_type=F32,
            )
        outp[pl.ds(2 * row, 2)] = grad.reshape(2, 64, 384).astype(BF16)
        for b in range(2):
            to = 2 * row + (b if turn > 0 else 1 - z % 2)
            if turn == 0 and b == 1:
                continue
            copy = remote(
                outp.at[to], in4.at[slot], s4.at[2 * turn + b], r4.at[slot],
                ((to // 2) * NZ + (z // 2) * 2 + to % 2, head),
            )
            copy.start()
            block_copies.append(copy)
    pltpu.make_async_copy(outp.at[slot], in4.at[slot], r4.at[slot]).start()

    div_1[...] = jnp.broadcast_to(jnp.sum(tiles, axis=0, keepdims=True), (8, 128))
    pltpu.make_async_copy(div_1, div_x.at[head], rx.at[head]).start()
    div_copies = [remote(div_1, div_x.at[head], sx.at[d], rx.at[head], (seq, (head + d) % 8)) for d in range(1, 8)]
    for copy in div_copies:
        copy.start()

    total = jnp.zeros((64, 384), F32)
    for n in range(8):
        pltpu.make_async_copy(in4.at[n], in4.at[n], r4.at[n]).wait()
        total = total + in4[n].astype(F32)
    win[...] = total.astype(BF16)
    lasts = [remote(win, prev, sw, rw, ahead), remote(win, follow, sv, rv, behind)]
    for copy in lasts:
        copy.start()
    both[:, 384:768] = win[...]
    for copy in block_copies + div_copies:
        copy.wait_send()

    @pl.when(active)
    def _():
        across.wait_send()
        for copy in row_copies:
            copy.wait_send()

    for p in range(2):
        @pl.when(pair_at(z, p) < PAIRS)
        def _():
            each_pair_copy(p, False)

    total = jnp.zeros((8, 128), F32)
    for n in range(8):
        pltpu.make_async_copy(div_x.at[n], div_x.at[n], rx.at[n]).wait()
        total = total + div_x[n]
    mean[0, 0] = jnp.sum(total[0:1]) * jnp.float32(1.0 / 196608.0)
    for copy in lasts:
        copy.wait_send()
        copy.wait_recv()
    both[:, 0:384] = prev[...]
    both[:, 768:1152] = follow[...]


def fold(part, cols):
    vmem = pl.BlockSpec(memory_space=pltpu.VMEM)
    smem = pl.BlockSpec(memory_space=pltpu.SMEM)
    dma = pltpu.SemaphoreType.DMA
    return pl.pallas_call(
        fold_kernel,
        name="fold",
        out_shape=(jax.ShapeDtypeStruct((1, 1), F32), jax.ShapeDtypeStruct((64, 1152), BF16)),
        in_specs=[pl.BlockSpec(memory_space=pl.ANY)] * 2,
        out_specs=(smem, vmem),
        scratch_shapes=[
            pltpu.VMEM((NY, PART, 128), BF16),
            pltpu.VMEM((NY, PART, 128), BF16),
            pltpu.VMEM((NY, PART, 128), BF16),
            pltpu.VMEM((NY, PART, 128), BF16),
            pltpu.VMEM((2, PART, 128), BF16),
            pltpu.VMEM((NZ, PART, 128), BF16),
            pltpu.VMEM((8, 64, 384), BF16),
            pltpu.VMEM((8, 64, 384), BF16),
            pltpu.VMEM((64, 384), BF16),
            pltpu.VMEM((64, 384), BF16),
            pltpu.VMEM((64, 384), BF16),
            pltpu.VMEM((8, 8, 128), F32),
            pltpu.VMEM((8, 128), F32),
            pltpu.VMEM((8, 4, 64, TOK), BF16),
            dma(()), dma(()), dma(()), dma(()), dma((NY,)), dma((NY,)), dma((8,)), dma((NZ,)), dma((8,)), dma((8,)),
            dma(()), dma(()), dma(()), dma(()), dma((8,)), dma((8,)),
        ],
        compiler_params=pltpu.CompilerParams(
            collective_id=1, has_side_effects=True, vmem_limit_bytes=VMEM_LIMIT
        ),
    )(part, cols)


def shift_kernel(s_shift, both, gq, gk, gv):
    there = lax.broadcasted_iota(jnp.int32, (384, 128), 0)
    here = lax.broadcasted_iota(jnp.int32, (384, 128), 1)
    pick = jnp.where(there == here + (192 - s_shift[0]), jnp.float32(1.0), jnp.float32(0.0)).astype(BF16)
    for kind, out in enumerate((gq, gk, gv)):
        out[...] = functools.reduce(
            jnp.add,
            [
                jnp.dot(
                    both[:, 384 * n + 128 * kind : 384 * n + 128 * kind + 128],
                    pick[128 * n : 128 * n + 128],
                    preferred_element_type=F32,
                )
                for n in range(3)
            ],
        ).astype(BF16)


def shift(s_shift, both):
    vmem = pl.BlockSpec(memory_space=pltpu.VMEM)
    grad = jax.ShapeDtypeStruct((64, 128), BF16)
    return pl.pallas_call(
        shift_kernel,
        name="shift",
        out_shape=(grad, grad, grad),
        in_specs=[pl.BlockSpec(memory_space=pltpu.SMEM), vmem],
        out_specs=(vmem, vmem, vmem),
    )(s_shift, both)


def local(
    teacher_query, teacher_key, teacher_value, student_hidden, weight_query, weight_key, weight_value,
    teacher_shift, student_shift, segment_lengths,
):
    keys, cols = spread(
        teacher_shift, student_shift, teacher_query, teacher_key, teacher_value, student_hidden,
        weight_query, weight_key, weight_value,
    )
    mean, both = fold(relate(segment_lengths, keys), cols)
    return (mean[0, 0], *shift(student_shift, both))


def solution(mesh):
    in_specs = (
        P("seq", "head"),
        P("seq", "head"),
        P("seq", "head"),
        P("seq", None),
        P(None, "head"),
        P(None, "head"),
        P(None, "head"),
        P(),
        P(),
        P(),
    )
    out_specs = (P(), P("seq", "head"), P("seq", "head"), P("seq", "head"))
    return jax.shard_map(local, mesh=mesh, in_specs=in_specs, out_specs=out_specs, check_vma=False)
```
